128 devices in a mesh: bundle: 64 (over x, y, z), elem: 2 (over core).
Axes of the slice: x: 4, y: 4, z: 4, core: 2. Of those that a mesh axis runs over, the one named last changes fastest.
Arguments:
- volt_start: float32 [16384, 2048], P(('bundle', 'elem')), may hold values from -6 to 6
- seg_ids: int32 [16384, 2048], P(('bundle', 'elem')), may hold values from 0 to 7, never falling along the last dimension, each value on 1 to 512 neighbouring positions
- cond_table: float32 [8], replicated, may hold values from 0.05 to 0.45
- tile_owner: int32 [262144, 1], P(('bundle', 'elem')), may hold values from 0 to 127; in each aligned block of 2048 rows (0 to 2047, 2048 to 4095, ...) at most 32 rows name the same one
- tile_elem: int32 [262144], P(('bundle', 'elem')), may hold values from 0 to 511
- material: bfloat16 [128, 128], replicated, may hold values from -0.1875 to 0.1875
- stress_cot: float32 [65536, 128], P(('bundle', 'elem')), may hold values from -6 to 6
Outputs:
- volt_grad: float32 [16384, 2048], P(('bundle', 'elem'))
- stress: float32 [65536, 128], P(('bundle', 'elem'))
- material_grad: float32 [128, 128], replicated
- cond_grad: float32 [8], replicated
The draws below stay inside these ranges and needn't reach their ends.
Inputs may be any that keep to these rules, and one draw needn't show every extreme that they name: `tile_owner`: in the rows of one device (aligned blocks of 2048 rows) no owner is named more than 32 times, a bound that some block reaches. `seg_ids`: never falls along a fiber; a segment spans at most 512 nodes.
All inputs are finite; a program needn't handle non-finite values.
Results may differ from the reference program's by a relative error of at most 0.0048.
Values may be sent and summed in bfloat16 or wider, within the bound.
No kernel may reach another device: no remote copies, remote signals or barrier semaphores. Data moves between devices by JAX's collectives and lax.ppermute only.
A program may use at most 64 MiB of HBM per device.

```python
import math
import jax
import jax.numpy as jnp
import numpy as np
from jax import lax

FIB_DEV = 128
NODES = 2048
TILE = 128
SEGS = 8
E_DEV = 512
STEPS = 4
TILES = 16
OWNERS = 128
FIBERS = 16384
ELEMS = 65536
CAP = 32


def with_ends(drawn, own_key, least, high):
    dims = drawn.shape
    spot = [jax.random.randint(jax.random.fold_in(own_key, axis), (), 0, dims[axis]) for axis in range(len(dims))]
    drawn = drawn.at[tuple(spot)].set(least)
    longest = dims.index(max(dims))
    spot[longest] = (spot[longest] + 1) % dims[longest]
    return drawn.at[tuple(spot)].set(high)


def steps_of(stream_key, shape, split, least, largest):
    gain, own = 1.0, jax.random.fold_in(stream_key, 6)
    for dim, shards_of in split:
        draws = jnp.exp(jax.random.uniform(jax.random.fold_in(own, dim), (shards_of,), jnp.float32, least / len(split), largest / len(split)))
        gain = gain * jnp.repeat(draws, shape[dim] // shards_of).reshape([-1 if axis == dim else 1 for axis in range(len(shape))])
    return gain


def split_up(number_of, total, bound, skew):
    portions = [(1 << 20) // math.isqrt(standing ** skew) + 1 for standing in range(2, number_of + 1)]
    spare, holding = total - bound - (number_of - 1), [1] * (number_of - 1)
    while spare > 0:
        candidates = [i for i in range(number_of - 1) if holding[i] < bound]
        mass, remaining = sum([portions[i] for i in candidates]), spare
        for i in candidates:
            extra = min(bound - holding[i], max(1, remaining * portions[i] // mass), spare)
            holding[i] = holding[i] + extra
            spare = spare - extra
    return np.array([bound] + holding)


def uneven_parts(own_key, number_of, total, bound, skew):
    if number_of == 2:
        one = jax.random.randint(own_key, (), max(1, total - bound), min(bound, total - 1) + 1)
        return jnp.stack([one, total - one])
    lengths = jnp.asarray(split_up(number_of, total, bound, skew), jnp.int32)
    pairs = (number_of - 1) // 2
    giver, receiver = lengths[1:1 + 2 * pairs:2], lengths[2:2 + 2 * pairs:2]
    margin = jnp.minimum(giver - 1, bound - receiver)
    shifted = jax.random.randint(jax.random.fold_in(own_key, 1), (pairs,), 0, 1 << 20) % (margin + 1)
    lengths = lengths.at[1:1 + 2 * pairs:2].set(giver - shifted).at[2:2 + 2 * pairs:2].set(receiver + shifted)
    return lengths[jax.random.permutation(jax.random.fold_in(own_key, 2), number_of)]


def deal_out(key, own, number, rows, count, top, reach, lean):
    order = jax.random.permutation(key, count)
    packed, usual = portions_of(count, rows * top, reach, lean, True), portions_of(count, rows * top, reach, lean, False)
    places = jnp.arange(count)

    def named(tallies, turn):
        used = int((tallies > 0).sum())
        fixed = max(1, used // 4)
        moved = fixed + (places - fixed + turn * (used - fixed)) % max(1, count - fixed)
        return jnp.zeros((count,), jnp.int32).at[order[jnp.where(places < fixed, places, moved)]].set(jnp.asarray(tallies, jnp.int32))

    tallies = jnp.where(number % 4 == 0, named(packed, number // 4), named(usual, number - number // 4 - 1))
    mixed = jax.random.permutation(jax.random.fold_in(own, 3), count)
    donor, receiver = mixed[0:count // 2 * 2:2], mixed[1:count // 2 * 2:2]
    room = jnp.minimum(tallies[donor] - 1, reach - tallies[receiver]) // 2
    room = jnp.where((donor == order[0]) | (receiver == order[0]) | (tallies[receiver] == 0), 0, jnp.maximum(room, 0))
    moved = jax.random.randint(jax.random.fold_in(own, 4), (count // 2,), 0, 1 << 20) % (room + 1)
    tallies = tallies.at[donor].add(-moved).at[receiver].add(moved)
    labels = jnp.searchsorted(jnp.cumsum(tallies), jnp.arange(rows * top), side="right").astype(jnp.int32)
    listing = labels.reshape(top, rows).T
    listing = listing[jax.random.permutation(jax.random.fold_in(own, 1), rows)]
    turn = jax.random.randint(jax.random.fold_in(own, 2), (rows, 1), 0, top)
    return jnp.take_along_axis(listing, (jnp.arange(top)[None, :] + turn) % top, axis=1)


def portions_of(count, total, most, lean, full):
    portions = [(1 << 20) // math.isqrt(standing ** lean) + 1 for standing in range(1, count + 1)]
    largest = most if full else min(most, max(-(-total // count), total * portions[0] // sum(portions)))
    least = 1 if total - largest >= count - 1 else 0
    given, spare = [largest] + [least] * (count - 1), total - largest - least * (count - 1)
    while spare > 0:
        free = [i for i in range(1, count) if given[i] < largest] or [i for i in range(1, count) if given[i] < most]
        whole, remaining = sum([portions[i] for i in free]), spare
        for i in free:
            extra = min(most - given[i], max(1, remaining * portions[i] // whole), spare)
            given[i] = given[i] + extra
            spare = spare - extra
    return np.array(given)


def bell_draw(own_key, extent, scale, most, shards=(), held_as=jnp.bfloat16):
    values = scale * jax.random.normal(own_key, extent, jnp.float32)
    if shards:
        values = values * steps_of(own_key, extent, shards, -0.22, 0.18)
    return jnp.clip(values, -most, most).astype(held_as)


def setup_inputs(seed: int = 0) -> dict:
    key_list = jax.random.split(jax.random.key(seed), 8)
    volt_start = bell_draw(key_list[0], (FIBERS, NODES), 1.0, 6.0, ((0, 128),), jnp.float32)
    seg_ids = jax.vmap(lambda own: jnp.searchsorted(jnp.cumsum(uneven_parts(own, SEGS, NODES, NODES // 4, 0)), jnp.arange(NODES), side="right"))(jax.random.split(key_list[1], FIBERS)).reshape((FIBERS, NODES)).astype(jnp.int32)
    cond_table = jnp.clip(jnp.exp(jax.random.uniform(key_list[2], (SEGS,), jnp.float32, math.log(0.05), math.log(0.45))), 0.05, 0.45)
    tile_owner_keys = jax.random.split(jax.random.fold_in(key_list[3], 1), (FIBERS * TILES) // (FIB_DEV * TILES))
    tile_owner_turns = jax.random.permutation(jax.random.fold_in(key_list[3], 3), (FIBERS * TILES) // (FIB_DEV * TILES))
    tile_owner = jax.vmap(lambda own, number: deal_out(jax.random.fold_in(key_list[3], 2), own, number, FIB_DEV * TILES, OWNERS, 1, CAP, 2))(tile_owner_keys, tile_owner_turns).reshape((FIBERS * TILES, 1))
    tile_elem = with_ends(jax.random.randint(key_list[4], (FIBERS * TILES,), 0, E_DEV), jax.random.fold_in(key_list[4], 1), 0, E_DEV - 1).astype(jnp.int32)
    material = bell_draw(key_list[5], (TILE, TILE), (8 * TILE) ** -0.5, 0.1875)
    stress_cot = bell_draw(key_list[6], (ELEMS, TILE), 1.0, 6.0, ((0, 128),), jnp.float32)
    return {"volt_start": volt_start, "seg_ids": seg_ids, "cond_table": cond_table, "tile_owner": tile_owner, "tile_elem": tile_elem, "material": material, "stress_cot": stress_cot}


time_step = 0.5
react_gain = 1.5

def fiber_step(volts, condn):
    left = jnp.concatenate([volts[:, :1], volts[:, :-1]], axis=1)
    right = jnp.concatenate([volts[:, 1:], volts[:, -1:]], axis=1)
    return volts + time_step * (condn * (left - 2.0 * volts + right) + jnp.tanh(react_gain * volts) - volts)

def reference(volt_start, seg_ids, cond_table, tile_owner, tile_elem, material, stress_cot):
    condn = cond_table[seg_ids]

    def forward(volts, conds):
        for index in range(STEPS):
            volts = fiber_step(volts, conds)
        return volts
    v_end, puller = jax.vjp(forward, volt_start, condn)
    act = jnp.tanh(v_end).astype(jnp.bfloat16)
    gid = (tile_owner[:, 0] * E_DEV + tile_elem).astype(jnp.int32)
    summed = jax.ops.segment_sum(act.reshape(-1, TILE).astype(jnp.float32), gid, num_segments=ELEMS)
    summed_b = summed.astype(jnp.bfloat16)
    stress = jnp.tanh(jnp.dot(summed_b, material, preferred_element_type=jnp.float32))
    gpre = stress_cot * (1.0 - stress * stress)
    gsum = jnp.dot(gpre, material.astype(jnp.float32).T, precision=lax.Precision.HIGHEST)
    material_grad = jnp.dot(summed_b.astype(jnp.float32).T, gpre, precision=lax.Precision.HIGHEST)
    tanh_end = jnp.tanh(v_end)
    g_end = gsum[gid].reshape(v_end.shape) * (1.0 - tanh_end * tanh_end)
    volt_grad, condn_grad = puller(g_end)
    cond_grad = jax.ops.segment_sum(condn_grad.reshape(-1), seg_ids.reshape(-1), num_segments=SEGS)
    return (volt_grad, stress, material_grad, cond_grad)
```

```python
import jax
import jax.numpy as jnp
from jax import lax
from jax.experimental import pallas as pl
from jax.experimental.pallas import tpu as pltpu
from jax.sharding import PartitionSpec as P

SEGS = 8
STEPS = 4
LANES = 128
FIB = 128
NODES = 2048
TILES = NODES // LANES
GROUPS = FIB // 8
OWNERS = 128
CAP = 32
ROWS = 40
ELEMS = 512
AXES = ("bundle", "elem")
F32 = jnp.float32
BF16 = jnp.bfloat16
NONE = -1000.0


def iota(shape, dim):
    return lax.broadcasted_iota(jnp.int32, shape, dim)


def dot(a, b):
    return jnp.dot(a, b, preferred_element_type=F32)


def dot_nt(a, b):
    return lax.dot_general(a, b, (((1,), (1,)), ((), ())), preferred_element_type=F32)


def dot_tn(a, b):
    return lax.dot_general(a, b, (((0,), (0,)), ((), ())), preferred_element_type=F32)


def onehot(mask):
    return jnp.where(mask, 1.0, 0.0)


def cut(rows):
    return [rows[:, j * LANES : (j + 1) * LANES] for j in range(TILES)]


def laplace(v, lane):
    from_left = [pltpu.roll(x, 1, axis=1) for x in v]
    from_right = [pltpu.roll(x, LANES - 1, axis=1) for x in v]
    out = []
    for j in range(TILES):
        left = jnp.where(lane == 0, from_left[j - 1] if j else v[0], from_left[j])
        right = jnp.where(
            lane == LANES - 1, from_right[j + 1] if j < TILES - 1 else v[j], from_right[j]
        )
        out.append(left + right - 2.0 * v[j])
    return out


def half_cond(seg, table):
    c = jnp.full(seg.shape, 0.5 * table[0], F32)
    for s in range(1, SEGS):
        c = jnp.where(seg == s, 0.5 * table[s], c)
    return c


def forward_kernel(table, volt, seg, owner, elem, send, qt, act):
    lane = iota((8, LANES), 1)

    def fibers(g, carry):
        rows = pl.ds(pl.multiple_of(g * 8, 8), 8)
        v = cut(volt[rows, :])
        c = cut(half_cond(seg[rows, :], table))
        for _ in range(STEPS):
            lap = laplace(v, lane)
            v = [0.5 * (x + jnp.tanh(1.5 * x)) + k * d for x, k, d in zip(v, c, lap)]
        tiles = jnp.concatenate([jnp.tanh(x) for x in v], axis=0)
        act[pl.ds(pl.multiple_of(g * LANES, LANES), LANES), :] = tiles.astype(BF16)
        return carry

    lax.fori_loop(0, GROUPS, fibers, 0)

    sub, lan = iota((LANES, LANES), 0), iota((LANES, LANES), 1)
    number = elem[...]
    raw = jnp.concatenate([owner[...], number & 255, (number >> 8) + 1], axis=0)
    order = onehot(sub == (lan % 8) * TILES + lan // 8).astype(BF16)
    ordered = dot(raw.astype(F32).astype(BF16), order)
    before = jnp.concatenate([onehot(sub < lan), jnp.ones((LANES, LANES), F32)], axis=1)
    before = before.astype(BF16)
    sub_f = sub.astype(F32)
    place = (sub % CAP).astype(F32)
    which = (sub // CAP).astype(F32)
    count = jnp.zeros((LANES, LANES), F32)
    ids = jnp.zeros((2 * OWNERS, LANES), F32)
    for b in range(GROUPS):
        own = ordered[b : b + 1, :]
        low = ordered[GROUPS + b : GROUPS + b + 1, :]
        high = ordered[2 * GROUPS + b : 2 * GROUPS + b + 1, :]
        mine = onehot(sub_f == own)
        counted = dot(mine.astype(BF16), before)
        rank = jnp.sum(mine * (counted[:, :LANES] + count), axis=0, keepdims=True)
        count = count + counted[:, LANES:]
        at_rank = place == rank
        qt[:, b * LANES : (b + 1) * LANES] = jnp.where(at_rank, own - which, NONE).astype(BF16)
        named = jnp.concatenate([mine * low, mine * high], axis=0).astype(BF16)
        ids = ids + dot_nt(named, onehot(at_rank).astype(BF16))

    row = iota((OWNERS, 8, LANES), 1)
    low_rows = jnp.broadcast_to(ids[:OWNERS][:, None, :], row.shape)
    high_rows = jnp.broadcast_to(ids[OWNERS:][:, None, :], row.shape)
    tail = jnp.where(row == 0, low_rows, jnp.where(row == 1, high_rows, 0.0))
    send[:, CAP:, :] = tail.astype(BF16)

    def slots(m, carry):
        parts = []
        for c in range(4):
            want = jnp.full((1, 1), 16 * m + 4 * c, jnp.int32).astype(F32).astype(BF16)
            parts.append(jnp.where(qt[...] == want, BF16(1), BF16(0)))
        rows = dot(jnp.concatenate(parts, axis=0), act[...]).astype(BF16)
        send[pl.ds(16 * m, 16), :CAP, :] = rows.reshape(16, CAP, LANES)
        return carry

    lax.fori_loop(0, OWNERS // 16, slots, 0)


def residual_kernel(table, volt, seg, qt, res, q):
    lane = iota((8, LANES), 1)

    def fibers(g, carry):
        rows = pl.ds(pl.multiple_of(g * 8, 8), 8)
        v = cut(volt[rows, :])
        c = cut(half_cond(seg[rows, :], table))
        for j in range(TILES):
            res[0, rows, j * LANES : (j + 1) * LANES] = c[j]
        for k in range(STEPS):
            lap = laplace(v, lane)
            new = []
            for j in range(TILES):
                t = jnp.tanh(1.5 * v[j])
                new.append(0.5 * (v[j] + t) + c[j] * lap[j])
                cols = slice(j * LANES, (j + 1) * LANES)
                res[2 + k, rows, cols] = lap[j]
                res[2 + STEPS + k, rows, cols] = 1.25 - 0.75 * t * t
            v = new
        for j in range(TILES):
            t = jnp.tanh(v[j])
            res[1, rows, j * LANES : (j + 1) * LANES] = 1.0 - t * t
        return carry

    lax.fori_loop(0, GROUPS, fibers, 0)
    for b in range(GROUPS):
        cols = slice(b * LANES, (b + 1) * LANES)
        q[cols, :] = qt[:, cols].astype(F32).T.astype(BF16)


def split_two(x):
    high = x.astype(BF16)
    return high, (x - high.astype(F32)).astype(BF16)


def element_kernel(got, cot, material, stress, back, key_row, key_col, gsum_b):
    row = iota((OWNERS, 8, LANES), 1)
    src = iota((OWNERS, 8, LANES), 0)
    lan3 = iota((OWNERS, 8, LANES), 2)
    mine = src % 4 == lan3 // CAP
    tail = got[:, CAP:, :].astype(F32)
    low = jnp.where(mine & (row == 0), tail, 0.0).astype(BF16).reshape(OWNERS * 8, LANES)
    high = jnp.where(mine & (row == 1), tail, 0.0).astype(BF16).reshape(OWNERS * 8, LANES)
    pick = onehot(iota((32, OWNERS * 8), 1) // 32 == iota((32, OWNERS * 8), 0)).astype(BF16)
    low_q = dot(pick, low)
    high_q = dot(pick, high)
    sums = []
    col = iota((256, LANES), 0).astype(F32).astype(BF16)
    slots = got[:, :CAP, :].reshape(OWNERS * CAP, LANES)
    for h in range(2):
        keys = jnp.where(high_q == h + 1, low_q, -1.0).astype(BF16)
        hit = [jnp.where(col == keys[q : q + 1, :], BF16(1), BF16(0)) for q in range(32)]
        sums.append(dot(jnp.concatenate(hit, axis=1), slots))
    summed = jnp.concatenate(sums, axis=0).astype(BF16)
    out = jnp.tanh(dot(summed, material[...]))
    stress[...] = out
    gpre = cot[...] * (1.0 - out * out)
    g_high, g_low = split_two(gpre)
    gsum_b[...] = (dot_nt(g_high, material[...]) + dot_nt(g_low, material[...])).astype(BF16)
    local = dot_tn(summed, g_high) + dot_tn(summed, g_low)
    l_high = local.astype(BF16).astype(F32)
    l_low = local - l_high
    high_rows = jnp.broadcast_to(l_high[:, None, :], row.shape)
    low_rows = jnp.broadcast_to(l_low[:, None, :], row.shape)
    back[:, CAP:, :] = jnp.where(
        row == 0, high_rows, jnp.where(row == 1, low_rows, 0.0)
    ).astype(BF16)

    key_row[...] = jnp.concatenate([low_q, high_q], axis=0)
    diagonal = iota((LANES, LANES), 0) == iota((LANES, LANES), 1)
    weigh = jnp.where(iota((2 * LANES, LANES), 0) < LANES, 1.0, 256.0).astype(BF16)
    lane = iota((1, LANES), 1).astype(F32).astype(BF16)
    for m in range(8):
        blocks = []
        for q in range(4 * m, 4 * m + 4):
            lo = jnp.where(diagonal, key_row[q : q + 1, :], 0.0)
            hi = jnp.where(diagonal, key_row[32 + q : 33 + q, :], 0.0)
            blocks.append(jnp.concatenate([lo, hi], axis=1).astype(BF16))
        key = dot(jnp.concatenate(blocks, axis=0), weigh)
        hits = []
        for c in range(4):
            part = (key - (256.0 + 128.0 * c)).astype(BF16)
            hits.append(jnp.where(part == lane, BF16(1), BF16(0)))
        rows = dot(jnp.concatenate(hits, axis=1), gsum_b[...]).astype(BF16)
        back[16 * m : 16 * m + 16, :CAP, :] = rows.reshape(16, CAP, LANES)


def adjoint_kernel(got, q, res, seg, volt_grad, last, grads, sums):
    sums[...] = jnp.zeros(sums.shape, F32)
    lane = iota((8, LANES), 1)

    def gather(m, carry):
        rows = pl.ds(pl.multiple_of(m * 512, 512), 512)
        mine = q[rows, :]
        hits = [jnp.where(mine == BF16(4 * c), BF16(1), BF16(0)) for c in range(32)]
        slots = got[:, :CAP, :].reshape(OWNERS * CAP, LANES)
        grads[rows, :] = dot(jnp.concatenate(hits, axis=1), slots)
        return carry

    lax.fori_loop(0, 4, gather, 0)

    def fibers(g, carry):
        rows = pl.ds(pl.multiple_of(g * 8, 8), 8)
        base = pl.multiple_of(g * LANES, LANES)
        scale = cut(res[1, rows, :])
        c = cut(res[0, rows, :])
        grad = [grads[pl.ds(base + 8 * j, 8), :] * scale[j] for j in range(TILES)]
        total = [jnp.zeros((8, LANES), F32)] * TILES
        for k in reversed(range(STEPS)):
            lap = cut(res[2 + k, rows, :])
            own = cut(res[2 + STEPS + k, rows, :])
            total = [t + x * d for t, x, d in zip(total, grad, lap)]
            spread = laplace([x * y for x, y in zip(grad, c)], lane)
            grad = [x * y + z for x, y, z in zip(grad, own, spread)]
        ids = cut(seg[rows, :])
        for j in range(TILES):
            volt_grad[rows, j * LANES : (j + 1) * LANES] = grad[j]
        for s in range(SEGS):
            part = jnp.where(ids[0] == s, total[0], 0.0)
            for j in range(1, TILES):
                part = part + jnp.where(ids[j] == s, total[j], 0.0)
            sums[s * 8 : s * 8 + 8, :] += part
        return carry

    lax.fori_loop(0, GROUPS, fibers, 0)
    mat = jnp.sum(got[:, CAP:, :].astype(F32), axis=0)
    mat = jnp.sum(mat[:2, :], axis=0, keepdims=True)
    lane1 = iota((1, LANES), 1)
    cond = jnp.zeros((1, LANES), F32)
    for s in range(SEGS):
        cond = jnp.where(lane1 == s, 0.5 * jnp.sum(sums[s * 8 : s * 8 + 8, :]), cond)
    both = jnp.concatenate([mat, cond], axis=0)
    last[...] = jnp.broadcast_to(both[None], last.shape)


VMEM = pl.BlockSpec(memory_space=pltpu.VMEM)
SMEM = pl.BlockSpec(memory_space=pltpu.SMEM)


def call(kernel, ins, outs, scratch, name, flops, moved, limit=48):
    return pl.pallas_call(
        kernel,
        in_specs=ins,
        out_specs=[VMEM] * len(outs),
        out_shape=[jax.ShapeDtypeStruct(s, t) for s, t in outs],
        scratch_shapes=scratch,
        compiler_params=pltpu.CompilerParams(vmem_limit_bytes=limit * 2**20),
        cost_estimate=pl.CostEstimate(flops=flops, bytes_accessed=moved, transcendentals=0),
        name=name,
    )


def exchange(x):
    return lax.all_to_all(x, AXES, split_axis=0, concat_axis=0, tiled=True)


def per_device(volt_start, seg_ids, cond_table, tile_owner, tile_elem, material, stress_cot):
    message = (OWNERS, ROWS, LANES)
    owner = tile_owner.reshape(GROUPS, LANES)
    elem = tile_elem.reshape(GROUPS, LANES)
    send, qt = call(
        forward_kernel,
        [SMEM] + [VMEM] * 4,
        [(message, BF16), ((LANES, NODES), BF16)],
        [pltpu.VMEM((NODES, LANES), BF16)],
        "forward",
        2 * 4096 * 2048 * 128,
        5 << 20,
    )(cond_table, volt_start, seg_ids, owner, elem)
    got = exchange(send)
    res, q = call(
        residual_kernel,
        [SMEM] + [VMEM] * 3,
        [((2 + 2 * STEPS, FIB, NODES), F32), ((NODES, LANES), BF16)],
        [],
        "residuals",
        1 << 28,
        14 << 20,
    )(cond_table, volt_start, seg_ids, qt)
    stress, back = call(
        element_kernel,
        [VMEM] * 3,
        [((ELEMS, LANES), F32), (message, BF16)],
        [
            pltpu.VMEM((64, LANES), F32),
            pltpu.VMEM((8, LANES), F32),
            pltpu.VMEM((ELEMS, LANES), BF16),
        ],
        "elements",
        1 << 31,
        4 << 20,
    )(got, stress_cot, material)
    got_back = exchange(back)
    volt_grad, last = call(
        adjoint_kernel,
        [VMEM] * 4,
        [((FIB, NODES), F32), ((OWNERS, 2, LANES), F32)],
        [pltpu.VMEM((NODES, LANES), F32), pltpu.VMEM((SEGS * 8, LANES), F32)],
        "adjoint",
        2 * 4096 * 2048 * 128,
        14 << 20,
    )(got_back, q, res, seg_ids)
    ends = exchange(last)
    return volt_grad, stress, ends[:, 0, :], jnp.sum(ends[:, 1, :SEGS], axis=0)


def solution(mesh):
    rows = P(AXES, None)
    return jax.shard_map(
        per_device,
        mesh=mesh,
        in_specs=(rows, rows, P(), rows, P(AXES), P(), rows),
        out_specs=(rows, rows, P(), P()),
        check_vma=False,
    )
```

```python
import jax
import jax.numpy as jnp
from jax import lax
from jax.experimental import pallas as pl
from jax.experimental.pallas import tpu as pltpu
from jax.sharding import PartitionSpec as P

SEGS = 8
STEPS = 4
LANES = 128
FIB = 128
NODES = 2048
TILES = NODES // LANES
GROUPS = FIB // 8
OWNERS = 128
CAP = 32
ROWS = 40
ELEMS = 512
AXES = ("bundle", "elem")
F32 = jnp.float32
BF16 = jnp.bfloat16
PART = 32
RAISE = 2.0**56
TINY = 1e-37


def iota(shape, dim):
    return lax.broadcasted_iota(jnp.int32, shape, dim)


def dot(a, b):
    return jnp.dot(a, b, preferred_element_type=F32)


def dot_nt(a, b):
    return lax.dot_general(a, b, (((1,), (1,)), ((), ())), preferred_element_type=F32)


def dot_tn(a, b):
    return lax.dot_general(a, b, (((0,), (0,)), ((), ())), preferred_element_type=F32)


def onehot(mask):
    return jnp.where(mask, 1.0, 0.0)


def cut(rows):
    return [rows[:, j * LANES : (j + 1) * LANES] for j in range(TILES)]


def neighbours(v, lane):
    from_left = [pltpu.roll(x, 1, axis=1) for x in v]
    from_right = [pltpu.roll(x, LANES - 1, axis=1) for x in v]
    out = []
    for j in range(TILES):
        left = jnp.where(lane == 0, from_left[j - 1] if j else v[0], from_left[j])
        right = jnp.where(
            lane == LANES - 1, from_right[j + 1] if j < TILES - 1 else v[j], from_right[j]
        )
        out.append(left + right)
    return out


def half_cond(seg, table):
    c = jnp.full(seg.shape, 0.5 * table[0], F32)
    for s in range(1, SEGS):
        c = jnp.where(seg == s, 0.5 * table[s], c)
    return c


def start_all(pairs, sems):
    copies = [pltpu.make_async_copy(a, b, sems.at[i]) for i, (a, b) in enumerate(pairs)]
    for c in copies:
        c.start()
    return copies


def columns(j):
    return slice(j * LANES, (j + 1) * LANES)


def forward_kernel(
    table_h, volt_h, seg_h, owner_h, elem_h, send, slots,
    table, volt, seg, owner, elem, act, stage, slot_s, sems, slot_sem,
):
    copies = start_all(
        [(owner_h, owner), (elem_h, elem), (table_h, table), (volt_h, volt), (seg_h, seg)], sems
    )
    stage[...] = jnp.zeros(stage.shape, F32)
    copies[0].wait()
    copies[1].wait()

    sub, lan = iota((LANES, LANES), 0), iota((LANES, LANES), 1)
    before = jnp.concatenate([onehot(sub < lan), jnp.ones((LANES, LANES), F32)], axis=1)
    before = before.astype(BF16)
    sub_f = sub.astype(F32)
    place = (sub % CAP).astype(F32)
    own_f = owner[...].astype(F32)
    low_f = (elem[...] & 255).astype(F32)
    high_f = ((elem[...] >> 8) + 1).astype(F32)
    count = jnp.zeros((LANES, LANES), F32)
    ids = jnp.zeros((2 * OWNERS, LANES), F32)
    for b in range(GROUPS):
        mine = onehot(sub_f == own_f[b : b + 1, :])
        counted = dot(mine.astype(BF16), before)
        rank = jnp.sum(mine * (counted[:, :LANES] + count), axis=0, keepdims=True)
        count = count + counted[:, LANES:]
        slots[b : b + 1, :] = (own_f[b : b + 1, :] * CAP + rank).astype(jnp.int32)
        named = [mine * low_f[b : b + 1, :], mine * high_f[b : b + 1, :]]
        named = jnp.concatenate(named, axis=0).astype(BF16)
        ids = ids + dot_nt(named, onehot(place == rank).astype(BF16))
    slot_copy = pltpu.make_async_copy(slots, slot_s, slot_sem)
    slot_copy.start()

    row = iota((OWNERS, 8, LANES), 1)
    low_rows = jnp.broadcast_to(ids[:OWNERS][:, None, :], row.shape)
    high_rows = jnp.broadcast_to(ids[OWNERS:][:, None, :], row.shape)
    tail = jnp.where(row == 0, low_rows, jnp.where(row == 1, high_rows, 0.0))
    send[:, CAP:, :] = tail.astype(BF16)
    for c in copies[2:]:
        c.wait()

    lane = iota((PART, LANES), 1)

    def fibers(g):
        rows = slice(g * PART, (g + 1) * PART)
        v = [1.5 * x for x in cut(volt[rows, :])]
        c = cut(half_cond(seg[rows, :], table))
        own = [0.5 - 2.0 * x for x in c]
        for _ in range(STEPS):
            both = neighbours(v, lane)
            v = [
                x * a + 0.75 * jnp.tanh(x) + k * y for x, a, k, y in zip(v, own, c, both)
            ]
        for j in range(TILES):
            act[rows, columns(j)] = jnp.tanh(v[j] * (1.0 / 1.5))

    def scatter(g):
        for f in range(g * PART, (g + 1) * PART):
            for j in range(TILES):
                slot = slot_s[f // 8, f % 8 * TILES + j]
                stage[pl.ds(slot, 1), :] = act[f : f + 1, columns(j)]

    fibers(0)
    slot_copy.wait()
    for g in range(1, FIB // PART):
        scatter(g - 1)
        fibers(g)
    scatter(FIB // PART - 1)
    for m in range(8):
        rows = stage[512 * m : 512 * (m + 1), :].astype(BF16)
        send[16 * m : 16 * (m + 1), :CAP, :] = rows.reshape(16, CAP, LANES)


def residual_kernel(table_h, volt_h, seg_h, res, table, volt, seg, sems):
    for c in start_all([(table_h, table), (volt_h, volt), (seg_h, seg)], sems):
        c.wait()
    lane = iota((PART, LANES), 1)

    def fibers(g, carry):
        rows = pl.ds(pl.multiple_of(g * PART, PART), PART)
        v = cut(volt[rows, :])
        c = cut(half_cond(seg[rows, :], table))
        for j in range(TILES):
            res[0, rows, columns(j)] = c[j]
        for k in range(STEPS):
            both = neighbours(v, lane)
            new = []
            for j in range(TILES):
                t = jnp.tanh(1.5 * v[j])
                lap = both[j] - 2.0 * v[j]
                new.append(0.5 * (v[j] + t) + c[j] * lap)
                res[2 + k, rows, columns(j)] = lap
                res[2 + STEPS + k, rows, columns(j)] = 1.25 - 0.75 * t * t - 2.0 * c[j]
            v = new
        for j in range(TILES):
            t = jnp.tanh(v[j])
            res[1, rows, columns(j)] = (1.0 - t * t) * (1.0 / RAISE)
        return carry

    lax.fori_loop(0, FIB // PART, fibers, 0)


def split_two(x):
    high = x.astype(BF16)
    return high, (x - high.astype(F32)).astype(BF16)


def element_kernel(got, cot, material, stress, back, key_row, key_col, gsum_b):
    row = iota((OWNERS, 8, LANES), 1)
    src = iota((OWNERS, 8, LANES), 0)
    lan3 = iota((OWNERS, 8, LANES), 2)
    mine = src % 4 == lan3 // CAP
    tail = got[:, CAP:, :].astype(F32)
    low = jnp.where(mine & (row == 0), tail, 0.0).astype(BF16).reshape(OWNERS * 8, LANES)
    high = jnp.where(mine & (row == 1), tail, 0.0).astype(BF16).reshape(OWNERS * 8, LANES)
    pick = onehot(iota((32, OWNERS * 8), 1) // 32 == iota((32, OWNERS * 8), 0)).astype(BF16)
    low_q = dot(pick, low)
    high_q = dot(pick, high)
    sums = []
    col = iota((256, LANES), 0).astype(F32).astype(BF16)
    slots = got[:, :CAP, :].reshape(OWNERS * CAP, LANES)
    for h in range(2):
        keys = jnp.where(high_q == h + 1, low_q, -1.0).astype(BF16)
        hit = [jnp.where(col == keys[q : q + 1, :], BF16(1), BF16(0)) for q in range(32)]
        sums.append(dot(jnp.concatenate(hit, axis=1), slots))
    summed = jnp.concatenate(sums, axis=0).astype(BF16)
    out = jnp.tanh(dot(summed, material[...]))
    stress[...] = out
    gpre = cot[...] * (1.0 - out * out)
    g_high, g_low = split_two(gpre)
    raised = (dot_nt(g_high, material[...]) + dot_nt(g_low, material[...])) * RAISE
    gsum_b[...] = (raised * jnp.abs(raised)).astype(BF16)
    local = dot_tn(summed, g_high) + dot_tn(summed, g_low)
    l_high = local.astype(BF16).astype(F32)
    l_low = local - l_high
    high_rows = jnp.broadcast_to(l_high[:, None, :], row.shape)
    low_rows = jnp.broadcast_to(l_low[:, None, :], row.shape)
    back[:, CAP:, :] = jnp.where(
        row == 0, high_rows, jnp.where(row == 1, low_rows, 0.0)
    ).astype(BF16)

    key_row[...] = jnp.concatenate([low_q, high_q], axis=0)
    diagonal = iota((LANES, LANES), 0) == iota((LANES, LANES), 1)
    weigh = jnp.where(iota((2 * LANES, LANES), 0) < LANES, 1.0, 256.0).astype(BF16)
    lane = iota((1, LANES), 1).astype(F32).astype(BF16)
    for m in range(8):
        blocks = []
        for q in range(4 * m, 4 * m + 4):
            lo = jnp.where(diagonal, key_row[q : q + 1, :], 0.0)
            hi = jnp.where(diagonal, key_row[32 + q : 33 + q, :], 0.0)
            blocks.append(jnp.concatenate([lo, hi], axis=1).astype(BF16))
        key = dot(jnp.concatenate(blocks, axis=0), weigh)
        hits = []
        for c in range(4):
            part = (key - (256.0 + 128.0 * c)).astype(BF16)
            hits.append(jnp.where(part == lane, BF16(1), BF16(0)))
        rows = dot(jnp.concatenate(hits, axis=1), gsum_b[...]).astype(BF16)
        back[16 * m : 16 * m + 16, :CAP, :] = rows.reshape(16, CAP, LANES)


def adjoint_kernel(
    got, slots_h, res, seg_h, volt_grad, last, rows_s, grads, sums, slot_s, seg, sems
):
    copies = start_all([(slots_h, slot_s), (seg_h, seg)], sems)
    for m in range(8):
        rows = got[16 * m : 16 * (m + 1), :CAP, :].astype(F32)
        rows_s[512 * m : 512 * (m + 1), :] = rows.reshape(512, LANES)
    for c in copies:
        c.wait()
    lane = iota((PART, LANES), 1)

    def gather(g):
        for f in range(g * PART, (g + 1) * PART):
            for j in range(TILES):
                slot = slot_s[f // 8, f % 8 * TILES + j]
                grads[f : f + 1, columns(j)] = rows_s[pl.ds(slot, 1), :]

    def fibers(g):
        rows = slice(g * PART, (g + 1) * PART)
        coded = cut(grads[rows, :])
        c = cut(res[0, rows, :])
        scale = cut(res[1, rows, :])
        grad = [
            x * lax.rsqrt(jnp.maximum(jnp.abs(x), TINY)) * y for x, y in zip(coded, scale)
        ]
        total = [jnp.zeros((PART, LANES), F32)] * TILES
        for k in reversed(range(STEPS)):
            lap = cut(res[2 + k, rows, :])
            own = cut(res[2 + STEPS + k, rows, :])
            total = [t + x * d for t, x, d in zip(total, grad, lap)]
            both = neighbours([x * y for x, y in zip(grad, c)], lane)
            grad = [x * y + z for x, y, z in zip(grad, own, both)]
        ids = cut(seg[rows, :])
        for j in range(TILES):
            volt_grad[rows, columns(j)] = grad[j]
        for s in range(SEGS):
            part = jnp.where(ids[0] == s, total[0], 0.0)
            for j in range(1, TILES):
                part = part + jnp.where(ids[j] == s, total[j], 0.0)
            part = jnp.sum(part.reshape(PART // 8, 8, LANES), axis=0)
            if g:
                part = part + sums[s * 8 : s * 8 + 8, :]
            sums[s * 8 : s * 8 + 8, :] = part

    gather(0)
    for g in range(FIB // PART):
        if g + 1 < FIB // PART:
            gather(g + 1)
        fibers(g)
    mat = jnp.sum(got[:, CAP:, :].astype(F32), axis=0)
    mat = jnp.sum(mat[:2, :], axis=0, keepdims=True)
    part = jnp.sum(sums[...].reshape(SEGS, 8, LANES), axis=1)
    part = 0.5 * jnp.sum(part, axis=1, keepdims=True)
    spot = iota((SEGS, LANES), 0) == iota((SEGS, LANES), 1)
    cond = jnp.sum(jnp.where(spot, part, 0.0), axis=0, keepdims=True)
    both = jnp.concatenate([mat, cond], axis=0)
    last[...] = jnp.broadcast_to(both[None], last.shape)


VMEM = pl.BlockSpec(memory_space=pltpu.VMEM)
HBM = pl.BlockSpec(memory_space=pltpu.HBM)


def call(kernel, ins, outs, scratch, name, flops, moved, limit=48):
    return pl.pallas_call(
        kernel,
        in_specs=ins,
        out_specs=[VMEM] * len(outs),
        out_shape=[jax.ShapeDtypeStruct(s, t) for s, t in outs],
        scratch_shapes=scratch,
        compiler_params=pltpu.CompilerParams(vmem_limit_bytes=limit * 2**20),
        cost_estimate=pl.CostEstimate(flops=flops, bytes_accessed=moved, transcendentals=0),
        name=name,
    )


def exchange(x):
    return lax.all_to_all(x, AXES, split_axis=0, concat_axis=0, tiled=True)


def per_device(volt_start, seg_ids, cond_table, tile_owner, tile_elem, material, stress_cot):
    message = (OWNERS, ROWS, LANES)
    owner = tile_owner.reshape(GROUPS, LANES)
    elem = tile_elem.reshape(GROUPS, LANES)
    fibers = (FIB, NODES)
    index = (GROUPS, LANES)
    send, slots = call(
        forward_kernel,
        [HBM] * 5,
        [(message, BF16), (index, jnp.int32)],
        [
            pltpu.SMEM((SEGS,), F32),
            pltpu.VMEM(fibers, F32),
            pltpu.VMEM(fibers, jnp.int32),
            pltpu.VMEM(index, jnp.int32),
            pltpu.VMEM(index, jnp.int32),
            pltpu.VMEM(fibers, F32),
            pltpu.VMEM((OWNERS * CAP, LANES), F32),
            pltpu.SMEM(index, jnp.int32),
            pltpu.SemaphoreType.DMA((5,)),
            pltpu.SemaphoreType.DMA,
        ],
        "forward",
        1 << 28,
        5 << 20,
    )(cond_table, volt_start, seg_ids, owner, elem)
    got = exchange(send)
    res = call(
        residual_kernel,
        [HBM] * 3,
        [((2 + 2 * STEPS, FIB, NODES), F32)],
        [
            pltpu.SMEM((SEGS,), F32),
            pltpu.VMEM(fibers, F32),
            pltpu.VMEM(fibers, jnp.int32),
            pltpu.SemaphoreType.DMA((3,)),
        ],
        "residuals",
        1 << 28,
        14 << 20,
    )(cond_table, volt_start, seg_ids)[0]
    stress, back = call(
        element_kernel,
        [VMEM] * 3,
        [((ELEMS, LANES), F32), (message, BF16)],
        [
            pltpu.VMEM((64, LANES), F32),
            pltpu.VMEM((8, LANES), F32),
            pltpu.VMEM((ELEMS, LANES), BF16),
        ],
        "elements",
        1 << 31,
        4 << 20,
    )(got, stress_cot, material)
    got_back = exchange(back)
    volt_grad, last = call(
        adjoint_kernel,
        [VMEM, HBM, VMEM, HBM],
        [(fibers, F32), ((OWNERS, 2, LANES), F32)],
        [
            pltpu.VMEM((OWNERS * CAP, LANES), F32),
            pltpu.VMEM(fibers, F32),
            pltpu.VMEM((SEGS * 8, LANES), F32),
            pltpu.SMEM(index, jnp.int32),
            pltpu.VMEM(fibers, jnp.int32),
            pltpu.SemaphoreType.DMA((2,)),
        ],
        "adjoint",
        1 << 28,
        14 << 20,
    )(got_back, slots, res, seg_ids)
    ends = exchange(last)
    return volt_grad, stress, ends[:, 0, :], jnp.sum(ends[:, 1, :SEGS], axis=0)


def solution(mesh):
    rows = P(AXES, None)
    return jax.shard_map(
        per_device,
        mesh=mesh,
        in_specs=(rows, rows, P(), rows, P(AXES), P(), rows),
        out_specs=(rows, rows, P(), P()),
        check_vma=False,
    )
```

```python
import jax
import jax.numpy as jnp
from jax import lax
from jax.experimental import pallas as pl
from jax.experimental.pallas import tpu as pltpu
from jax.sharding import PartitionSpec as P

SEGS = 8
STEPS = 4
LANES = 128
FIB = 128
NODES = 2048
TILES = NODES // LANES
GROUPS = FIB // 8
OWNERS = 128
CAP = 32
ROWS = 40
ELEMS = 512
AXES = ("bundle", "elem")
F32 = jnp.float32
BF16 = jnp.bfloat16
PART = 32
CHUNKS = 4
RAISE = 2.0**56
TINY = 1e-37


def iota(shape, dim):
    return lax.broadcasted_iota(jnp.int32, shape, dim)


def dot(a, b):
    return jnp.dot(a, b, preferred_element_type=F32)


def dot_nt(a, b):
    return lax.dot_general(a, b, (((1,), (1,)), ((), ())), preferred_element_type=F32)


def dot_tn(a, b):
    return lax.dot_general(a, b, (((0,), (0,)), ((), ())), preferred_element_type=F32)


def onehot(mask):
    return jnp.where(mask, 1.0, 0.0)


def cut(rows):
    return [rows[:, j * LANES : (j + 1) * LANES] for j in range(TILES)]


def neighbours(v, lane):
    from_left = [pltpu.roll(x, 1, axis=1) for x in v]
    from_right = [pltpu.roll(x, LANES - 1, axis=1) for x in v]
    out = []
    for j in range(TILES):
        left = jnp.where(lane == 0, from_left[j - 1] if j else v[0], from_left[j])
        right = jnp.where(
            lane == LANES - 1, from_right[j + 1] if j < TILES - 1 else v[j], from_right[j]
        )
        out.append(left + right)
    return out


def half_cond(seg, table):
    c = jnp.full(seg.shape, 0.5 * table[0], F32)
    for s in range(1, SEGS):
        c = jnp.where(seg == s, 0.5 * table[s], c)
    return c


def start_all(pairs, sems):
    copies = [pltpu.make_async_copy(a, b, sems.at[i]) for i, (a, b) in enumerate(pairs)]
    for c in copies:
        c.start()
    return copies


def columns(j):
    return slice(j * LANES, (j + 1) * LANES)


def forward_kernel(
    table_h, volt_h, seg_h, owner_h, elem_h, send, slots,
    table, volt, seg, owner, elem, act, stage, slot_s, sems, slot_sem,
):
    copies = start_all(
        [(owner_h, owner), (elem_h, elem), (table_h, table), (volt_h, volt), (seg_h, seg)], sems
    )
    stage[...] = jnp.zeros(stage.shape, F32)
    copies[0].wait()
    copies[1].wait()

    sub, lan = iota((LANES, LANES), 0), iota((LANES, LANES), 1)
    before = jnp.concatenate([onehot(sub < lan), jnp.ones((LANES, LANES), F32)], axis=1)
    before = before.astype(BF16)
    sub_f = sub.astype(F32)
    place = (sub % CAP).astype(F32)
    own_f = owner[...].astype(F32)
    low_f = (elem[...] & 255).astype(F32)
    high_f = ((elem[...] >> 8) + 1).astype(F32)
    count = jnp.zeros((LANES, LANES), F32)
    ids = jnp.zeros((2 * OWNERS, LANES), F32)
    for b in range(GROUPS):
        mine = onehot(sub_f == own_f[b : b + 1, :])
        counted = dot(mine.astype(BF16), before)
        rank = jnp.sum(mine * (counted[:, :LANES] + count), axis=0, keepdims=True)
        count = count + counted[:, LANES:]
        slots[b : b + 1, :] = (own_f[b : b + 1, :] * CAP + rank).astype(jnp.int32)
        named = [mine * low_f[b : b + 1, :], mine * high_f[b : b + 1, :]]
        named = jnp.concatenate(named, axis=0).astype(BF16)
        ids = ids + dot_nt(named, onehot(place == rank).astype(BF16))
    slot_copy = pltpu.make_async_copy(slots, slot_s, slot_sem)
    slot_copy.start()

    row = iota((OWNERS, 8, LANES), 1)
    low_rows = jnp.broadcast_to(ids[:OWNERS][:, None, :], row.shape)
    high_rows = jnp.broadcast_to(ids[OWNERS:][:, None, :], row.shape)
    tail = jnp.where(row == 0, low_rows, jnp.where(row == 1, high_rows, 0.0))
    send[:, CAP:, :] = tail.astype(BF16)
    for c in copies[2:]:
        c.wait()

    lane = iota((PART, LANES), 1)

    def fibers(g):
        rows = slice(g * PART, (g + 1) * PART)
        v = [1.5 * x for x in cut(volt[rows, :])]
        c = cut(half_cond(seg[rows, :], table))
        own = [0.5 - 2.0 * x for x in c]
        for _ in range(STEPS):
            both = neighbours(v, lane)
            v = [
                x * a + 0.75 * jnp.tanh(x) + k * y for x, a, k, y in zip(v, own, c, both)
            ]
        for j in range(TILES):
            act[rows, columns(j)] = jnp.tanh(v[j] * (1.0 / 1.5))

    def scatter(g):
        for f in range(g * PART, (g + 1) * PART):
            for j in range(TILES):
                slot = slot_s[f // 8, f % 8 * TILES + j]
                stage[pl.ds(slot, 1), :] = act[f : f + 1, columns(j)]

    fibers(0)
    slot_copy.wait()
    for g in range(1, FIB // PART):
        scatter(g - 1)
        fibers(g)
    scatter(FIB // PART - 1)
    leave = []
    for m in range(CHUNKS):
        some = slice(m * OWNERS // CHUNKS, (m + 1) * OWNERS // CHUNKS)
        rows = stage[CAP * some.start : CAP * some.stop, :].astype(BF16)
        send[some, :CAP, :] = rows.reshape(-1, CAP, LANES)


def residual_kernel(table_h, volt_h, seg_h, res, table, volt, seg, sems):
    for c in start_all([(table_h, table), (volt_h, volt), (seg_h, seg)], sems):
        c.wait()
    lane = iota((PART, LANES), 1)

    def fibers(g, carry):
        rows = pl.ds(pl.multiple_of(g * PART, PART), PART)
        v = cut(volt[rows, :])
        c = cut(half_cond(seg[rows, :], table))
        for j in range(TILES):
            res[0, rows, columns(j)] = c[j]
        for k in range(STEPS):
            both = neighbours(v, lane)
            new = []
            for j in range(TILES):
                t = jnp.tanh(1.5 * v[j])
                lap = both[j] - 2.0 * v[j]
                new.append(0.5 * (v[j] + t) + c[j] * lap)
                res[2 + k, rows, columns(j)] = lap
                res[2 + STEPS + k, rows, columns(j)] = 1.25 - 0.75 * t * t - 2.0 * c[j]
            v = new
        for j in range(TILES):
            t = jnp.tanh(v[j])
            res[1, rows, columns(j)] = (1.0 - t * t) * (1.0 / RAISE)
        return carry

    lax.fori_loop(0, FIB // PART, fibers, 0)


def split_two(x):
    high = x.astype(BF16)
    return high, (x - high.astype(F32)).astype(BF16)


def element_kernel(got, cot, material, stress, back, key_row, gsum_b):
    row = iota((OWNERS, 8, LANES), 1)
    src = iota((OWNERS, 8, LANES), 0)
    lan3 = iota((OWNERS, 8, LANES), 2)
    mine = src % 4 == lan3 // CAP
    tail = got[:, CAP:, :].astype(F32)
    low = jnp.where(mine & (row == 0), tail, 0.0).astype(BF16).reshape(OWNERS * 8, LANES)
    high = jnp.where(mine & (row == 1), tail, 0.0).astype(BF16).reshape(OWNERS * 8, LANES)
    pick = onehot(iota((32, OWNERS * 8), 1) // 32 == iota((32, OWNERS * 8), 0)).astype(BF16)
    low_q = dot(pick, low)
    high_q = dot(pick, high)
    sums = []
    col = iota((256, LANES), 0).astype(F32).astype(BF16)
    slots = got[:, :CAP, :].reshape(OWNERS * CAP, LANES)
    for h in range(2):
        keys = jnp.where(high_q == h + 1, low_q, -1.0).astype(BF16)
        hit = [jnp.where(col == keys[q : q + 1, :], BF16(1), BF16(0)) for q in range(32)]
        sums.append(dot(jnp.concatenate(hit, axis=1), slots))
    summed = jnp.concatenate(sums, axis=0).astype(BF16)
    out = jnp.tanh(dot(summed, material[...]))
    stress[...] = out
    gpre = cot[...] * (1.0 - out * out)
    g_high, g_low = split_two(gpre)
    raised = (dot_nt(g_high, material[...]) + dot_nt(g_low, material[...])) * RAISE
    gsum_b[...] = (raised * jnp.abs(raised)).astype(BF16)
    local = dot_tn(summed, g_high) + dot_tn(summed, g_low)
    l_high = local.astype(BF16).astype(F32)
    l_low = local - l_high
    high_rows = jnp.broadcast_to(l_high[:, None, :], row.shape)
    low_rows = jnp.broadcast_to(l_low[:, None, :], row.shape)
    back[:, CAP:, :] = jnp.where(
        row == 0, high_rows, jnp.where(row == 1, low_rows, 0.0)
    ).astype(BF16)

    key_row[...] = jnp.concatenate([low_q, high_q], axis=0)
    diagonal = iota((LANES, LANES), 0) == iota((LANES, LANES), 1)
    weigh = jnp.where(iota((2 * LANES, LANES), 0) < LANES, 1.0, 256.0).astype(BF16)
    lane = iota((1, LANES), 1).astype(F32).astype(BF16)
    leave = []
    for m in range(8):
        blocks = []
        for q in range(4 * m, 4 * m + 4):
            lo = jnp.where(diagonal, key_row[q : q + 1, :], 0.0)
            hi = jnp.where(diagonal, key_row[32 + q : 33 + q, :], 0.0)
            blocks.append(jnp.concatenate([lo, hi], axis=1).astype(BF16))
        key = dot(jnp.concatenate(blocks, axis=0), weigh)
        hits = []
        for c in range(4):
            part = (key - (256.0 + 128.0 * c)).astype(BF16)
            hits.append(jnp.where(part == lane, BF16(1), BF16(0)))
        rows = dot(jnp.concatenate(hits, axis=1), gsum_b[...]).astype(BF16)
        some = slice(16 * m, 16 * m + 16)
        back[some, :CAP, :] = rows.reshape(16, CAP, LANES)


def adjoint_kernel(
    got, slots_h, res_h, seg_h, volt_h, last,
    rows_s, grads, sums, slot_s, seg, res, volt_grad, sems, res_sems, out_sems,
):
    copies = start_all([(slots_h, slot_s), (seg_h, seg)], sems)
    parts = [slice(g * PART, (g + 1) * PART) for g in range(FIB // PART)]
    arrive = start_all([(res_h.at[:, p, :], res.at[:, p, :]) for p in parts], res_sems)
    for m in range(8):
        rows = got[16 * m : 16 * (m + 1), :CAP, :].astype(F32)
        rows_s[512 * m : 512 * (m + 1), :] = rows.reshape(512, LANES)
    for c in copies:
        c.wait()
    lane = iota((PART, LANES), 1)

    def gather(g):
        for f in range(g * PART, (g + 1) * PART):
            for j in range(TILES):
                slot = slot_s[f // 8, f % 8 * TILES + j]
                grads[f : f + 1, columns(j)] = rows_s[pl.ds(slot, 1), :]

    def fibers(g):
        rows = slice(g * PART, (g + 1) * PART)
        coded = cut(grads[rows, :])
        c = cut(res[0, rows, :])
        scale = cut(res[1, rows, :])
        grad = [
            x * lax.rsqrt(jnp.maximum(jnp.abs(x), TINY)) * y for x, y in zip(coded, scale)
        ]
        total = [jnp.zeros((PART, LANES), F32)] * TILES
        for k in reversed(range(STEPS)):
            lap = cut(res[2 + k, rows, :])
            own = cut(res[2 + STEPS + k, rows, :])
            total = [t + x * d for t, x, d in zip(total, grad, lap)]
            both = neighbours([x * y for x, y in zip(grad, c)], lane)
            grad = [x * y + z for x, y, z in zip(grad, own, both)]
        ids = cut(seg[rows, :])
        for j in range(TILES):
            volt_grad[rows, columns(j)] = grad[j]
        for s in range(SEGS):
            part = jnp.where(ids[0] == s, total[0], 0.0)
            for j in range(1, TILES):
                part = part + jnp.where(ids[j] == s, total[j], 0.0)
            part = jnp.sum(part.reshape(PART // 8, 8, LANES), axis=0)
            if g:
                part = part + sums[s * 8 : s * 8 + 8, :]
            sums[s * 8 : s * 8 + 8, :] = part

    gather(0)
    leave = []
    for g, p in enumerate(parts):
        arrive[g].wait()
        if g + 1 < FIB // PART:
            gather(g + 1)
        fibers(g)
        leave += start_all([(volt_grad.at[p], volt_h.at[p])], out_sems.at[g : g + 1])
    mat = jnp.sum(got[:, CAP:, :].astype(F32), axis=0)
    mat = jnp.sum(mat[:2, :], axis=0, keepdims=True)
    part = jnp.sum(sums[...].reshape(SEGS, 8, LANES), axis=1)
    part = 0.5 * jnp.sum(part, axis=1, keepdims=True)
    spot = iota((SEGS, LANES), 0) == iota((SEGS, LANES), 1)
    cond = jnp.sum(jnp.where(spot, part, 0.0), axis=0, keepdims=True)
    both = jnp.concatenate([mat, cond], axis=0)
    last[...] = jnp.broadcast_to(both[None], last.shape)
    for c in leave:
        c.wait()


def last_kernel(ends, material_grad, cond_grad):
    both = ends[...]
    material_grad[...] = both[:, 0, :]
    cond_grad[...] = jnp.sum(both, axis=0)[1, :SEGS]


VMEM = pl.BlockSpec(memory_space=pltpu.VMEM)
HBM = pl.BlockSpec(memory_space=pltpu.HBM)


def call(kernel, ins, outs, scratch, name, flops, moved, limit=48, where=None):
    return pl.pallas_call(
        kernel,
        in_specs=ins,
        out_specs=where or [VMEM] * len(outs),
        out_shape=[jax.ShapeDtypeStruct(s, t) for s, t in outs],
        scratch_shapes=scratch,
        compiler_params=pltpu.CompilerParams(vmem_limit_bytes=limit * 2**20),
        cost_estimate=pl.CostEstimate(flops=flops, bytes_accessed=moved, transcendentals=0),
        name=name,
    )


def exchange(x):
    return lax.all_to_all(x, AXES, split_axis=0, concat_axis=0, tiled=True)


def per_device(volt_start, seg_ids, cond_table, tile_owner, tile_elem, material, stress_cot):
    message = (OWNERS, ROWS, LANES)
    owner = tile_owner.reshape(GROUPS, LANES)
    elem = tile_elem.reshape(GROUPS, LANES)
    fibers = (FIB, NODES)
    index = (GROUPS, LANES)
    send, slots = call(
        forward_kernel,
        [HBM] * 5,
        [(message, BF16), (index, jnp.int32)],
        [
            pltpu.SMEM((SEGS,), F32),
            pltpu.VMEM(fibers, F32),
            pltpu.VMEM(fibers, jnp.int32),
            pltpu.VMEM(index, jnp.int32),
            pltpu.VMEM(index, jnp.int32),
            pltpu.VMEM(fibers, F32),
            pltpu.VMEM((OWNERS * CAP, LANES), F32),
            pltpu.SMEM(index, jnp.int32),
            pltpu.SemaphoreType.DMA((5,)),
            pltpu.SemaphoreType.DMA,
        ],
        "forward",
        1 << 28,
        5 << 20,
        60,
        [VMEM, VMEM],
    )(cond_table, volt_start, seg_ids, owner, elem)
    got = exchange(send)
    res = call(
        residual_kernel,
        [HBM] * 3,
        [((2 + 2 * STEPS, FIB, NODES), F32)],
        [
            pltpu.SMEM((SEGS,), F32),
            pltpu.VMEM(fibers, F32),
            pltpu.VMEM(fibers, jnp.int32),
            pltpu.SemaphoreType.DMA((3,)),
        ],
        "residuals",
        1 << 28,
        14 << 20,
    )(cond_table, volt_start, seg_ids)[0]
    stress, back = call(
        element_kernel,
        [VMEM] * 3,
        [((ELEMS, LANES), F32), (message, BF16)],
        [
            pltpu.VMEM((64, LANES), F32),
            pltpu.VMEM((ELEMS, LANES), BF16),
        ],
        "elements",
        1 << 31,
        4 << 20,
        32,
        [VMEM, VMEM],
    )(got, stress_cot, material)
    got_back = exchange(back)
    volt_grad, last = call(
        adjoint_kernel,
        [VMEM, HBM, HBM, HBM],
        [(fibers, F32), ((OWNERS, 2, LANES), F32)],
        [
            pltpu.VMEM((OWNERS * CAP, LANES), F32),
            pltpu.VMEM(fibers, F32),
            pltpu.VMEM((SEGS * 8, LANES), F32),
            pltpu.SMEM(index, jnp.int32),
            pltpu.VMEM(fibers, jnp.int32),
            pltpu.VMEM((2 + 2 * STEPS, *fibers), F32),
            pltpu.VMEM(fibers, F32),
            pltpu.SemaphoreType.DMA((2,)),
            pltpu.SemaphoreType.DMA((FIB // PART,)),
            pltpu.SemaphoreType.DMA((FIB // PART,)),
        ],
        "adjoint",
        1 << 28,
        14 << 20,
        48,
        [HBM, VMEM],
    )(got_back, slots, res, seg_ids)
    ends = exchange(last)
    material_grad, cond_grad = call(
        last_kernel,
        [VMEM],
        [((LANES, LANES), F32), ((SEGS,), F32)],
        [],
        "last_sums",
        1 << 16,
        1 << 17,
    )(ends)
    return volt_grad, stress, material_grad, cond_grad


def solution(mesh):
    rows = P(AXES, None)
    return jax.shard_map(
        per_device,
        mesh=mesh,
        in_specs=(rows, rows, P(), rows, P(AXES), P(), rows),
        out_specs=(rows, rows, P(), P()),
        check_vma=False,
    )
```

```python
import jax
import jax.numpy as jnp
from jax import lax
from jax.experimental import pallas as pl
from jax.experimental.pallas import tpu as pltpu
from jax.sharding import PartitionSpec as P

SEGS = 8
STEPS = 4
LANES = 128
FIB = 128
NODES = 2048
TILES = NODES // LANES
GROUPS = FIB // 8
OWNERS = 128
CAP = 32
ROWS = 40
ELEMS = 512
AXES = ("bundle", "elem")
F32 = jnp.float32
BF16 = jnp.bfloat16
PART = 32
CHUNKS = 4
RAISE = 2.0**56
TINY = 1e-37


def iota(shape, dim):
    return lax.broadcasted_iota(jnp.int32, shape, dim)


def dot(a, b):
    return jnp.dot(a, b, preferred_element_type=F32)


def dot_nt(a, b):
    return lax.dot_general(a, b, (((1,), (1,)), ((), ())), preferred_element_type=F32)


def dot_tn(a, b):
    return lax.dot_general(a, b, (((0,), (0,)), ((), ())), preferred_element_type=F32)


def onehot(mask):
    return jnp.where(mask, 1.0, 0.0)


def cut(rows):
    return [rows[:, j * LANES : (j + 1) * LANES] for j in range(TILES)]


def neighbours(v, lane):
    from_left = [pltpu.roll(x, 1, axis=1) for x in v]
    from_right = [pltpu.roll(x, LANES - 1, axis=1) for x in v]
    out = []
    for j in range(TILES):
        left = jnp.where(lane == 0, from_left[j - 1] if j else v[0], from_left[j])
        right = jnp.where(
            lane == LANES - 1, from_right[j + 1] if j < TILES - 1 else v[j], from_right[j]
        )
        out.append(left + right)
    return out


def half_cond(seg, table):
    c = jnp.full(seg.shape, 0.5 * table[0], F32)
    for s in range(1, SEGS):
        c = jnp.where(seg == s, 0.5 * table[s], c)
    return c


def start_all(pairs, sems):
    copies = [pltpu.make_async_copy(a, b, sems.at[i]) for i, (a, b) in enumerate(pairs)]
    for c in copies:
        c.start()
    return copies


def columns(j):
    return slice(j * LANES, (j + 1) * LANES)


def forward_kernel(
    table_h, volt_h, seg_h, owner_h, elem_h, send, slots,
    table, volt, seg, owner, elem, act, stage, slot_s, sems, slot_sem,
):
    parts = [slice(g * PART, (g + 1) * PART) for g in range(FIB // PART)]
    small = start_all([(owner_h, owner), (elem_h, elem), (table_h, table)], sems)
    large = start_all(
        [(a.at[p], b.at[p]) for p in parts for a, b in ((volt_h, volt), (seg_h, seg))],
        sems.at[3:],
    )
    stage[...] = jnp.zeros(stage.shape, F32)
    for c in small + large[:2]:
        c.wait()

    sub, lan = iota((LANES, LANES), 0), iota((LANES, LANES), 1)
    before = jnp.concatenate([onehot(sub < lan), jnp.ones((LANES, LANES), F32)], axis=1)
    before = before.astype(BF16)
    own_f = owner[...].astype(F32)
    own_b = own_f.astype(BF16)
    low_f = (elem[...] & 255).astype(F32)
    high_f = ((elem[...] >> 8) + 1).astype(F32)
    sub_b = sub.astype(F32).astype(BF16)
    place = iota((CAP, LANES), 0).astype(F32)
    count = jnp.zeros((LANES, LANES), F32)
    ids = jnp.zeros((OWNERS, 2 * CAP), F32)
    for b in range(GROUPS):
        mine = jnp.where(sub_b == own_b[b : b + 1, :], BF16(1), BF16(0))
        counted = dot(mine, before)
        rank = mine.astype(F32) * (counted[:, :LANES] + count)
        rank = jnp.sum(rank, axis=0, keepdims=True)
        count = count + counted[:, LANES:]
        slots[b : b + 1, :] = (own_f[b : b + 1, :] * CAP + rank).astype(jnp.int32)
        at_rank = place == rank
        named = [jnp.where(at_rank, x[b : b + 1, :], 0.0) for x in (low_f, high_f)]
        ids = ids + dot_nt(mine, jnp.concatenate(named, axis=0).astype(BF16))

    row = iota((OWNERS, 8, LANES), 1)
    again = iota((2 * CAP, 2 * LANES), 0), iota((2 * CAP, 2 * LANES), 1)
    again = again[0] == again[1] // LANES * CAP + again[1] % CAP
    ids = dot(ids.astype(BF16), onehot(again).astype(BF16))
    low_rows = jnp.broadcast_to(ids[:, None, :LANES], row.shape)
    high_rows = jnp.broadcast_to(ids[:, None, LANES:], row.shape)
    tail = jnp.where(row == 0, low_rows, jnp.where(row == 1, high_rows, 0.0))
    send[:, CAP:, :] = tail.astype(BF16)

    lane = iota((PART, LANES), 1)

    def fibers(g):
        rows = slice(g * PART, (g + 1) * PART)
        v = [1.5 * x for x in cut(volt[rows, :])]
        c = cut(half_cond(seg[rows, :], table))
        own = [0.5 - 2.0 * x for x in c]
        for _ in range(STEPS):
            both = neighbours(v, lane)
            v = [
                x * a + 0.75 * jnp.tanh(x) + k * y for x, a, k, y in zip(v, own, c, both)
            ]
        for j in range(TILES):
            act[rows, columns(j)] = jnp.tanh(v[j] * (1.0 / 1.5))

    def scatter(g):
        for f in range(g * PART, (g + 1) * PART):
            for j in range(TILES):
                slot = slot_s[f // 8, f % 8 * TILES + j]
                stage[pl.ds(slot, 1), :] = act[f : f + 1, columns(j)]

    fibers(0)
    slot_copy = pltpu.make_async_copy(slots, slot_s, slot_sem)
    slot_copy.start()
    for g in range(1, FIB // PART):
        for c in large[2 * g : 2 * g + 2]:
            c.wait()
        if g > 1:
            scatter(g - 2)
        fibers(g)
        if g == 1:
            slot_copy.wait()
    scatter(FIB // PART - 2)
    scatter(FIB // PART - 1)
    leave = []
    for m in range(CHUNKS):
        some = slice(m * OWNERS // CHUNKS, (m + 1) * OWNERS // CHUNKS)
        rows = stage[CAP * some.start : CAP * some.stop, :].astype(BF16)
        send[some, :CAP, :] = rows.reshape(-1, CAP, LANES)


def residual_kernel(table_h, volt_h, seg_h, res, table, volt, seg, sems):
    for c in start_all([(table_h, table), (volt_h, volt), (seg_h, seg)], sems):
        c.wait()
    lane = iota((PART, LANES), 1)

    def fibers(g, carry):
        rows = pl.ds(pl.multiple_of(g * PART, PART), PART)
        v = cut(volt[rows, :])
        c = cut(half_cond(seg[rows, :], table))
        for j in range(TILES):
            res[0, rows, columns(j)] = c[j]
        for k in range(STEPS):
            both = neighbours(v, lane)
            new = []
            for j in range(TILES):
                t = jnp.tanh(1.5 * v[j])
                lap = both[j] - 2.0 * v[j]
                new.append(0.5 * (v[j] + t) + c[j] * lap)
                res[2 + k, rows, columns(j)] = lap
                res[2 + STEPS + k, rows, columns(j)] = 1.25 - 0.75 * t * t - 2.0 * c[j]
            v = new
        for j in range(TILES):
            t = jnp.tanh(v[j])
            res[1, rows, columns(j)] = (1.0 - t * t) * (1.0 / RAISE)
        return carry

    lax.fori_loop(0, FIB // PART, fibers, 0)


def split_two(x):
    high = x.astype(BF16)
    return high, (x - high.astype(F32)).astype(BF16)


def element_kernel(got, cot, material, stress, back, key_row, gsum_b):
    row = iota((OWNERS, 8, LANES), 1)
    src = iota((OWNERS, 8, LANES), 0)
    lan3 = iota((OWNERS, 8, LANES), 2)
    mine = src % 4 == lan3 // CAP
    tail = got[:, CAP:, :].astype(F32)
    low = jnp.where(mine & (row == 0), tail, 0.0).astype(BF16).reshape(OWNERS * 8, LANES)
    high = jnp.where(mine & (row == 1), tail, 0.0).astype(BF16).reshape(OWNERS * 8, LANES)
    pick = onehot(iota((32, OWNERS * 8), 1) // 32 == iota((32, OWNERS * 8), 0)).astype(BF16)
    low_q = dot(pick, low)
    high_q = dot(pick, high)
    sums = []
    col = iota((256, LANES), 0).astype(F32).astype(BF16)
    slots = got[:, :CAP, :].reshape(OWNERS * CAP, LANES)
    for h in range(2):
        keys = jnp.where(high_q == h + 1, low_q, -1.0).astype(BF16)
        hit = [jnp.where(col == keys[q : q + 1, :], BF16(1), BF16(0)) for q in range(32)]
        sums.append(dot(jnp.concatenate(hit, axis=1), slots))
    summed = jnp.concatenate(sums, axis=0).astype(BF16)
    out = jnp.tanh(dot(summed, material[...]))
    stress[...] = out
    gpre = cot[...] * (1.0 - out * out)
    g_high, g_low = split_two(gpre)
    raised = (dot_nt(g_high, material[...]) + dot_nt(g_low, material[...])) * RAISE
    gsum_b[...] = (raised * jnp.abs(raised)).astype(BF16)
    local = dot_tn(summed, g_high) + dot_tn(summed, g_low)
    l_high = local.astype(BF16).astype(F32)
    l_low = local - l_high
    high_rows = jnp.broadcast_to(l_high[:, None, :], row.shape)
    low_rows = jnp.broadcast_to(l_low[:, None, :], row.shape)
    back[:, CAP:, :] = jnp.where(
        row == 0, high_rows, jnp.where(row == 1, low_rows, 0.0)
    ).astype(BF16)

    key_row[...] = jnp.concatenate([low_q, high_q], axis=0)
    diagonal = iota((LANES, LANES), 0) == iota((LANES, LANES), 1)
    weigh = jnp.where(iota((2 * LANES, LANES), 0) < LANES, 1.0, 256.0).astype(BF16)
    lane = iota((1, LANES), 1).astype(F32).astype(BF16)
    leave = []
    for m in range(8):
        blocks = []
        for q in range(4 * m, 4 * m + 4):
            lo = jnp.where(diagonal, key_row[q : q + 1, :], 0.0)
            hi = jnp.where(diagonal, key_row[32 + q : 33 + q, :], 0.0)
            blocks.append(jnp.concatenate([lo, hi], axis=1).astype(BF16))
        key = dot(jnp.concatenate(blocks, axis=0), weigh)
        hits = []
        for c in range(4):
            part = (key - (256.0 + 128.0 * c)).astype(BF16)
            hits.append(jnp.where(part == lane, BF16(1), BF16(0)))
        rows = dot(jnp.concatenate(hits, axis=1), gsum_b[...]).astype(BF16)
        some = slice(16 * m, 16 * m + 16)
        back[some, :CAP, :] = rows.reshape(16, CAP, LANES)


def adjoint_kernel(
    got, slots_h, res, seg_h, volt_h, last,
    rows_s, grads, sums, slot_s, seg, volt_grad, sems, out_sems,
):
    copies = start_all([(slots_h, slot_s), (seg_h, seg)], sems)
    parts = [slice(g * PART, (g + 1) * PART) for g in range(FIB // PART)]
    for m in range(8):
        rows = got[16 * m : 16 * (m + 1), :CAP, :].astype(F32)
        rows_s[512 * m : 512 * (m + 1), :] = rows.reshape(512, LANES)
    for c in copies:
        c.wait()
    lane = iota((PART, LANES), 1)

    def gather(g):
        for f in range(g * PART, (g + 1) * PART):
            for j in range(TILES):
                slot = slot_s[f // 8, f % 8 * TILES + j]
                grads[f : f + 1, columns(j)] = rows_s[pl.ds(slot, 1), :]

    def fibers(g):
        rows = slice(g * PART, (g + 1) * PART)
        coded = cut(grads[rows, :])
        c = cut(res[0, rows, :])
        scale = cut(res[1, rows, :])
        grad = [
            x * lax.rsqrt(jnp.maximum(jnp.abs(x), TINY)) * y for x, y in zip(coded, scale)
        ]
        total = [jnp.zeros((PART, LANES), F32)] * TILES
        for k in reversed(range(STEPS)):
            lap = cut(res[2 + k, rows, :])
            own = cut(res[2 + STEPS + k, rows, :])
            total = [t + x * d for t, x, d in zip(total, grad, lap)]
            both = neighbours([x * y for x, y in zip(grad, c)], lane)
            grad = [x * y + z for x, y, z in zip(grad, own, both)]
        ids = cut(seg[rows, :])
        for j in range(TILES):
            volt_grad[rows, columns(j)] = grad[j]
        for s in range(SEGS):
            part = jnp.where(ids[0] == s, total[0], 0.0)
            for j in range(1, TILES):
                part = part + jnp.where(ids[j] == s, total[j], 0.0)
            part = jnp.sum(part.reshape(PART // 8, 8, LANES), axis=0)
            if g:
                part = part + sums[s * 8 : s * 8 + 8, :]
            sums[s * 8 : s * 8 + 8, :] = part

    gather(0)
    leave = []
    for g, p in enumerate(parts):
        if g + 1 < FIB // PART:
            gather(g + 1)
        fibers(g)
        leave += start_all([(volt_grad.at[p], volt_h.at[p])], out_sems.at[g : g + 1])
    mat = jnp.sum(got[:, CAP:, :].astype(F32), axis=0)
    mat = jnp.sum(mat[:2, :], axis=0, keepdims=True)
    part = jnp.sum(sums[...].reshape(SEGS, 8, LANES), axis=1)
    part = 0.5 * jnp.sum(part, axis=1, keepdims=True)
    spot = iota((SEGS, LANES), 0) == iota((SEGS, LANES), 1)
    cond = jnp.sum(jnp.where(spot, part, 0.0), axis=0, keepdims=True)
    both = jnp.concatenate([mat, cond], axis=0)
    last[...] = jnp.broadcast_to(both[None], last.shape)
    for c in leave:
        c.wait()


def last_kernel(ends, material_grad, cond_grad):
    both = ends[...]
    material_grad[...] = both[:, 0, :]
    cond_grad[...] = jnp.sum(both, axis=0)[1, :SEGS]


VMEM = pl.BlockSpec(memory_space=pltpu.VMEM)
HBM = pl.BlockSpec(memory_space=pltpu.HBM)


def call(kernel, ins, outs, scratch, name, flops, moved, limit=48, where=None):
    return pl.pallas_call(
        kernel,
        in_specs=ins,
        out_specs=where or [VMEM] * len(outs),
        out_shape=[jax.ShapeDtypeStruct(s, t) for s, t in outs],
        scratch_shapes=scratch,
        compiler_params=pltpu.CompilerParams(vmem_limit_bytes=limit * 2**20),
        cost_estimate=pl.CostEstimate(flops=flops, bytes_accessed=moved, transcendentals=0),
        name=name,
    )


def exchange(x):
    return lax.all_to_all(x, AXES, split_axis=0, concat_axis=0, tiled=True)


def per_device(volt_start, seg_ids, cond_table, tile_owner, tile_elem, material, stress_cot):
    message = (OWNERS, ROWS, LANES)
    owner = tile_owner.reshape(GROUPS, LANES)
    elem = tile_elem.reshape(GROUPS, LANES)
    fibers = (FIB, NODES)
    index = (GROUPS, LANES)
    send, slots = call(
        forward_kernel,
        [HBM] * 5,
        [(message, BF16), (index, jnp.int32)],
        [
            pltpu.SMEM((SEGS,), F32),
            pltpu.VMEM(fibers, F32),
            pltpu.VMEM(fibers, jnp.int32),
            pltpu.VMEM(index, jnp.int32),
            pltpu.VMEM(index, jnp.int32),
            pltpu.VMEM(fibers, F32),
            pltpu.VMEM((OWNERS * CAP, LANES), F32),
            pltpu.SMEM(index, jnp.int32),
            pltpu.SemaphoreType.DMA((3 + 2 * (FIB // PART),)),
            pltpu.SemaphoreType.DMA,
        ],
        "forward",
        1 << 28,
        5 << 20,
        60,
        [VMEM, VMEM],
    )(cond_table, volt_start, seg_ids, owner, elem)
    got = exchange(send)
    res = call(
        residual_kernel,
        [HBM] * 3,
        [((2 + 2 * STEPS, FIB, NODES), F32)],
        [
            pltpu.SMEM((SEGS,), F32),
            pltpu.VMEM(fibers, F32),
            pltpu.VMEM(fibers, jnp.int32),
            pltpu.SemaphoreType.DMA((3,)),
        ],
        "residuals",
        1 << 28,
        14 << 20,
        24,
    )(cond_table, volt_start, seg_ids)[0]
    stress, back = call(
        element_kernel,
        [VMEM] * 3,
        [((ELEMS, LANES), F32), (message, BF16)],
        [
            pltpu.VMEM((64, LANES), F32),
            pltpu.VMEM((ELEMS, LANES), BF16),
        ],
        "elements",
        1 << 31,
        4 << 20,
        32,
        [VMEM, VMEM],
    )(got, stress_cot, material)
    got_back = exchange(back)
    volt_grad, last = call(
        adjoint_kernel,
        [VMEM, HBM, VMEM, HBM],
        [(fibers, F32), ((OWNERS, 2, LANES), F32)],
        [
            pltpu.VMEM((OWNERS * CAP, LANES), F32),
            pltpu.VMEM(fibers, F32),
            pltpu.VMEM((SEGS * 8, LANES), F32),
            pltpu.SMEM(index, jnp.int32),
            pltpu.VMEM(fibers, jnp.int32),
            pltpu.VMEM(fibers, F32),
            pltpu.SemaphoreType.DMA((2,)),
            pltpu.SemaphoreType.DMA((FIB // PART,)),
        ],
        "adjoint",
        1 << 28,
        14 << 20,
        24,
        [HBM, VMEM],
    )(got_back, slots, res, seg_ids)
    ends = exchange(last)
    material_grad, cond_grad = call(
        last_kernel,
        [VMEM],
        [((LANES, LANES), F32), ((SEGS,), F32)],
        [],
        "last_sums",
        1 << 16,
        1 << 17,
    )(ends)
    return volt_grad, stress, material_grad, cond_grad


def solution(mesh):
    rows = P(AXES, None)
    return jax.shard_map(
        per_device,
        mesh=mesh,
        in_specs=(rows, rows, P(), rows, P(AXES), P(), rows),
        out_specs=(rows, rows, P(), P()),
        check_vma=False,
    )
```

```python
import jax
import jax.numpy as jnp
from jax import lax
from jax.experimental import pallas as pl
from jax.experimental.pallas import tpu as pltpu
from jax.sharding import PartitionSpec as P

SEGS = 8
STEPS = 4
LANES = 128
FIB = 128
NODES = 2048
TILES = NODES // LANES
GROUPS = FIB // 8
OWNERS = 128
CAP = 32
ROWS = 40
ELEMS = 512
AXES = ("bundle", "elem")
F32 = jnp.float32
BF16 = jnp.bfloat16
PART = 32
CHUNKS = 4
RAISE = 2.0**56
TINY = 1e-37


def iota(shape, dim):
    return lax.broadcasted_iota(jnp.int32, shape, dim)


def dot(a, b):
    return jnp.dot(a, b, preferred_element_type=F32)


def dot_nt(a, b):
    return lax.dot_general(a, b, (((1,), (1,)), ((), ())), preferred_element_type=F32)


def dot_tn(a, b):
    return lax.dot_general(a, b, (((0,), (0,)), ((), ())), preferred_element_type=F32)


def onehot(mask):
    return jnp.where(mask, 1.0, 0.0)


def cut(rows):
    return [rows[:, j * LANES : (j + 1) * LANES] for j in range(TILES)]


def neighbours(v, lane):
    from_left = [pltpu.roll(x, 1, axis=1) for x in v]
    from_right = [pltpu.roll(x, LANES - 1, axis=1) for x in v]
    out = []
    for j in range(TILES):
        left = jnp.where(lane == 0, from_left[j - 1] if j else v[0], from_left[j])
        right = jnp.where(
            lane == LANES - 1, from_right[j + 1] if j < TILES - 1 else v[j], from_right[j]
        )
        out.append(left + right)
    return out


def half_cond(seg, table):
    c = jnp.full(seg.shape, 0.5 * table[0], F32)
    for s in range(1, SEGS):
        c = jnp.where(seg == s, 0.5 * table[s], c)
    return c


def start_all(pairs, sems):
    copies = [pltpu.make_async_copy(a, b, sems.at[i]) for i, (a, b) in enumerate(pairs)]
    for c in copies:
        c.start()
    return copies


def columns(j):
    return slice(j * LANES, (j + 1) * LANES)


def forward_kernel(
    table_h, volt_h, seg_h, owner_h, elem_h, send, slots,
    table, volt, seg, owner, elem, act, stage, slot_s, sems, slot_sem,
):
    parts = [slice(g * PART, (g + 1) * PART) for g in range(FIB // PART)]
    small = start_all([(owner_h, owner), (elem_h, elem), (table_h, table)], sems)
    large = start_all(
        [(a.at[p], b.at[p]) for p in parts for a, b in ((volt_h, volt), (seg_h, seg))],
        sems.at[3:],
    )
    stage[...] = jnp.zeros(stage.shape, F32)
    for c in small + large[:2]:
        c.wait()

    sub, lan = iota((LANES, LANES), 0), iota((LANES, LANES), 1)
    before = jnp.concatenate([onehot(sub < lan), jnp.ones((LANES, LANES), F32)], axis=1)
    before = before.astype(BF16)
    own_f = owner[...].astype(F32)
    own_b = own_f.astype(BF16)
    low_f = (elem[...] & 255).astype(F32)
    high_f = ((elem[...] >> 8) + 1).astype(F32)
    sub_b = sub.astype(F32).astype(BF16)
    place = iota((CAP, LANES), 0).astype(F32)
    count = jnp.zeros((LANES, LANES), F32)
    ids = jnp.zeros((OWNERS, 2 * CAP), F32)
    for b in range(GROUPS):
        mine = jnp.where(sub_b == own_b[b : b + 1, :], BF16(1), BF16(0))
        counted = dot(mine, before)
        rank = mine.astype(F32) * (counted[:, :LANES] + count)
        rank = jnp.sum(rank, axis=0, keepdims=True)
        count = count + counted[:, LANES:]
        slots[b : b + 1, :] = (own_f[b : b + 1, :] * CAP + rank).astype(jnp.int32)
        at_rank = place == rank
        named = [jnp.where(at_rank, x[b : b + 1, :], 0.0) for x in (low_f, high_f)]
        ids = ids + dot_nt(mine, jnp.concatenate(named, axis=0).astype(BF16))

    row = iota((OWNERS, 8, LANES), 1)
    again = iota((2 * CAP, 2 * LANES), 0), iota((2 * CAP, 2 * LANES), 1)
    again = again[0] == again[1] // LANES * CAP + again[1] % CAP
    ids = dot(ids.astype(BF16), onehot(again).astype(BF16))
    low_rows = jnp.broadcast_to(ids[:, None, :LANES], row.shape)
    high_rows = jnp.broadcast_to(ids[:, None, LANES:], row.shape)
    tail = jnp.where(row == 0, low_rows, jnp.where(row == 1, high_rows, 0.0))
    send[:, CAP:, :] = tail.astype(BF16)

    lane = iota((PART, LANES), 1)

    def fibers(g):
        rows = slice(g * PART, (g + 1) * PART)
        v = [1.5 * x for x in cut(volt[rows, :])]
        c = cut(half_cond(seg[rows, :], table))
        own = [0.5 - 2.0 * x for x in c]
        for _ in range(STEPS):
            both = neighbours(v, lane)
            v = [
                x * a + 0.75 * jnp.tanh(x) + k * y for x, a, k, y in zip(v, own, c, both)
            ]
        for j in range(TILES):
            act[rows, columns(j)] = jnp.tanh(v[j] * (1.0 / 1.5))

    def scatter(g):
        for f in range(g * PART, (g + 1) * PART):
            for j in range(TILES):
                slot = slot_s[f // 8, f % 8 * TILES + j]
                stage[pl.ds(slot, 1), :] = act[f : f + 1, columns(j)]

    fibers(0)
    slot_copy = pltpu.make_async_copy(slots, slot_s, slot_sem)
    slot_copy.start()
    for g in range(1, FIB // PART):
        for c in large[2 * g : 2 * g + 2]:
            c.wait()
        if g > 1:
            scatter(g - 2)
        fibers(g)
        if g == 1:
            slot_copy.wait()
    scatter(FIB // PART - 2)
    scatter(FIB // PART - 1)
    leave = []
    for m in range(CHUNKS):
        some = slice(m * OWNERS // CHUNKS, (m + 1) * OWNERS // CHUNKS)
        rows = stage[CAP * some.start : CAP * some.stop, :].astype(BF16)
        send[some, :CAP, :] = rows.reshape(-1, CAP, LANES)


def residual_kernel(table_h, volt_h, seg_h, cot_h, res, cot, table, volt, seg, sems):
    pairs = [(table_h, table), (volt_h, volt), (seg_h, seg), (cot_h, cot)]
    for c in start_all(pairs, sems):
        c.wait()
    lane = iota((PART, LANES), 1)

    def fibers(g, carry):
        rows = pl.ds(pl.multiple_of(g * PART, PART), PART)
        v = cut(volt[rows, :])
        c = cut(half_cond(seg[rows, :], table))
        for j in range(TILES):
            res[0, rows, columns(j)] = c[j]
        for k in range(STEPS):
            both = neighbours(v, lane)
            new = []
            for j in range(TILES):
                t = jnp.tanh(1.5 * v[j])
                lap = both[j] - 2.0 * v[j]
                new.append(0.5 * (v[j] + t) + c[j] * lap)
                res[2 + k, rows, columns(j)] = lap
                res[2 + STEPS + k, rows, columns(j)] = 1.25 - 0.75 * t * t - 2.0 * c[j]
            v = new
        for j in range(TILES):
            t = jnp.tanh(v[j])
            res[1, rows, columns(j)] = (1.0 - t * t) * (1.0 / RAISE)
        return carry

    lax.fori_loop(0, FIB // PART, fibers, 0)


def split_two(x):
    high = x.astype(BF16)
    return high, (x - high.astype(F32)).astype(BF16)


def element_kernel(got, cot, material, stress, back, key_row, gsum_b):
    row = iota((OWNERS, 8, LANES), 1)
    src = iota((OWNERS, 8, LANES), 0)
    lan3 = iota((OWNERS, 8, LANES), 2)
    mine = src % 4 == lan3 // CAP
    tail = got[:, CAP:, :].astype(F32)
    low = jnp.where(mine & (row == 0), tail, 0.0).astype(BF16).reshape(OWNERS * 8, LANES)
    high = jnp.where(mine & (row == 1), tail, 0.0).astype(BF16).reshape(OWNERS * 8, LANES)
    pick = onehot(iota((32, OWNERS * 8), 1) // 32 == iota((32, OWNERS * 8), 0)).astype(BF16)
    low_q = dot(pick, low)
    high_q = dot(pick, high)
    sums = []
    col = iota((256, LANES), 0).astype(F32).astype(BF16)
    slots = got[:, :CAP, :].reshape(OWNERS * CAP, LANES)
    for h in range(2):
        keys = jnp.where(high_q == h + 1, low_q, -1.0).astype(BF16)
        hit = [jnp.where(col == keys[q : q + 1, :], BF16(1), BF16(0)) for q in range(32)]
        sums.append(dot(jnp.concatenate(hit, axis=1), slots))
    summed = jnp.concatenate(sums, axis=0).astype(BF16)
    out = jnp.tanh(dot(summed, material[...]))
    stress[...] = out
    gpre = cot[...] * (1.0 - out * out)
    g_high, g_low = split_two(gpre)
    raised = (dot_nt(g_high, material[...]) + dot_nt(g_low, material[...])) * RAISE
    gsum_b[...] = (raised * jnp.abs(raised)).astype(BF16)
    local = dot_tn(summed, g_high) + dot_tn(summed, g_low)
    l_high = local.astype(BF16).astype(F32)
    l_low = local - l_high
    high_rows = jnp.broadcast_to(l_high[:, None, :], row.shape)
    low_rows = jnp.broadcast_to(l_low[:, None, :], row.shape)
    back[:, CAP:, :] = jnp.where(
        row == 0, high_rows, jnp.where(row == 1, low_rows, 0.0)
    ).astype(BF16)

    key_row[...] = jnp.concatenate([low_q, high_q], axis=0)
    diagonal = iota((LANES, LANES), 0) == iota((LANES, LANES), 1)
    weigh = jnp.where(iota((2 * LANES, LANES), 0) < LANES, 1.0, 256.0).astype(BF16)
    lane = iota((1, LANES), 1).astype(F32).astype(BF16)
    leave = []
    for m in range(8):
        blocks = []
        for q in range(4 * m, 4 * m + 4):
            lo = jnp.where(diagonal, key_row[q : q + 1, :], 0.0)
            hi = jnp.where(diagonal, key_row[32 + q : 33 + q, :], 0.0)
            blocks.append(jnp.concatenate([lo, hi], axis=1).astype(BF16))
        key = dot(jnp.concatenate(blocks, axis=0), weigh)
        hits = []
        for c in range(4):
            part = (key - (256.0 + 128.0 * c)).astype(BF16)
            hits.append(jnp.where(part == lane, BF16(1), BF16(0)))
        rows = dot(jnp.concatenate(hits, axis=1), gsum_b[...]).astype(BF16)
        some = slice(16 * m, 16 * m + 16)
        back[some, :CAP, :] = rows.reshape(16, CAP, LANES)


def adjoint_kernel(
    got, slots_h, res_h, seg_h, volt_h, last,
    rows_s, grads, sums, slot_s, seg, res, volt_grad, sems, res_sems, out_sems,
):
    copies = start_all([(slots_h, slot_s), (seg_h, seg)], sems)
    parts = [slice(g * PART, (g + 1) * PART) for g in range(FIB // PART)]
    arrive = start_all([(res_h.at[:, p, :], res.at[:, p, :]) for p in parts], res_sems)
    for m in range(8):
        rows = got[16 * m : 16 * (m + 1), :CAP, :].astype(F32)
        rows_s[512 * m : 512 * (m + 1), :] = rows.reshape(512, LANES)
    for c in copies:
        c.wait()
    lane = iota((PART, LANES), 1)

    def gather(g):
        for f in range(g * PART, (g + 1) * PART):
            for j in range(TILES):
                slot = slot_s[f // 8, f % 8 * TILES + j]
                grads[f : f + 1, columns(j)] = rows_s[pl.ds(slot, 1), :]

    def fibers(g):
        rows = slice(g * PART, (g + 1) * PART)
        coded = cut(grads[rows, :])
        c = cut(res[0, rows, :])
        scale = cut(res[1, rows, :])
        grad = [
            x * lax.rsqrt(jnp.maximum(jnp.abs(x), TINY)) * y for x, y in zip(coded, scale)
        ]
        total = [jnp.zeros((PART, LANES), F32)] * TILES
        for k in reversed(range(STEPS)):
            lap = cut(res[2 + k, rows, :])
            own = cut(res[2 + STEPS + k, rows, :])
            total = [t + x * d for t, x, d in zip(total, grad, lap)]
            both = neighbours([x * y for x, y in zip(grad, c)], lane)
            grad = [x * y + z for x, y, z in zip(grad, own, both)]
        ids = cut(seg[rows, :])
        for j in range(TILES):
            volt_grad[rows, columns(j)] = grad[j]
        for s in range(SEGS):
            part = jnp.where(ids[0] == s, total[0], 0.0)
            for j in range(1, TILES):
                part = part + jnp.where(ids[j] == s, total[j], 0.0)
            part = jnp.sum(part.reshape(PART // 8, 8, LANES), axis=0)
            if g:
                part = part + sums[s * 8 : s * 8 + 8, :]
            sums[s * 8 : s * 8 + 8, :] = part

    gather(0)
    gather(1)
    leave = []
    for g, p in enumerate(parts):
        arrive[g].wait()
        if g + 2 < FIB // PART:
            gather(g + 2)
        fibers(g)
        leave += start_all([(volt_grad.at[p], volt_h.at[p])], out_sems.at[g : g + 1])
    mat = jnp.sum(got[:, CAP:, :].astype(F32), axis=0)
    mat = jnp.sum(mat[:2, :], axis=0, keepdims=True)
    part = jnp.sum(sums[...].reshape(SEGS, 8, LANES), axis=1)
    part = 0.5 * jnp.sum(part, axis=1, keepdims=True)
    spot = iota((SEGS, LANES), 0) == iota((SEGS, LANES), 1)
    cond = jnp.sum(jnp.where(spot, part, 0.0), axis=0, keepdims=True)
    both = jnp.concatenate([mat, cond], axis=0)
    last[...] = jnp.broadcast_to(both[None], last.shape)
    for c in leave:
        c.wait()


def last_kernel(ends, material_grad, cond_grad):
    both = ends[...]
    material_grad[...] = both[:, 0, :]
    cond_grad[...] = jnp.sum(both, axis=0)[1, :SEGS]


VMEM = pl.BlockSpec(memory_space=pltpu.VMEM)
HBM = pl.BlockSpec(memory_space=pltpu.HBM)


def call(kernel, ins, outs, scratch, name, flops, moved, limit=48, where=None):
    return pl.pallas_call(
        kernel,
        in_specs=ins,
        out_specs=where or [VMEM] * len(outs),
        out_shape=[jax.ShapeDtypeStruct(s, t) for s, t in outs],
        scratch_shapes=scratch,
        compiler_params=pltpu.CompilerParams(vmem_limit_bytes=limit * 2**20),
        cost_estimate=pl.CostEstimate(flops=flops, bytes_accessed=moved, transcendentals=0),
        name=name,
    )


def exchange(x):
    return lax.all_to_all(x, AXES, split_axis=0, concat_axis=0, tiled=True)


def per_device(volt_start, seg_ids, cond_table, tile_owner, tile_elem, material, stress_cot):
    message = (OWNERS, ROWS, LANES)
    owner = tile_owner.reshape(GROUPS, LANES)
    elem = tile_elem.reshape(GROUPS, LANES)
    fibers = (FIB, NODES)
    index = (GROUPS, LANES)
    send, slots = call(
        forward_kernel,
        [HBM] * 5,
        [(message, BF16), (index, jnp.int32)],
        [
            pltpu.SMEM((SEGS,), F32),
            pltpu.VMEM(fibers, F32),
            pltpu.VMEM(fibers, jnp.int32),
            pltpu.VMEM(index, jnp.int32),
            pltpu.VMEM(index, jnp.int32),
            pltpu.VMEM(fibers, F32),
            pltpu.VMEM((OWNERS * CAP, LANES), F32),
            pltpu.SMEM(index, jnp.int32),
            pltpu.SemaphoreType.DMA((3 + 2 * (FIB // PART),)),
            pltpu.SemaphoreType.DMA,
        ],
        "forward",
        1 << 28,
        5 << 20,
        60,
        [VMEM, VMEM],
    )(cond_table, volt_start, seg_ids, owner, elem)
    got = exchange(send)
    res, cot = call(
        residual_kernel,
        [HBM] * 4,
        [((2 + 2 * STEPS, FIB, NODES), F32), ((ELEMS, LANES), F32)],
        [
            pltpu.SMEM((SEGS,), F32),
            pltpu.VMEM(fibers, F32),
            pltpu.VMEM(fibers, jnp.int32),
            pltpu.SemaphoreType.DMA((4,)),
        ],
        "residuals",
        1 << 28,
        14 << 20,
    )(cond_table, volt_start, seg_ids, stress_cot)
    stress, back = call(
        element_kernel,
        [VMEM] * 3,
        [((ELEMS, LANES), F32), (message, BF16)],
        [
            pltpu.VMEM((64, LANES), F32),
            pltpu.VMEM((ELEMS, LANES), BF16),
        ],
        "elements",
        1 << 31,
        4 << 20,
        32,
        [VMEM, VMEM],
    )(got, cot, material)
    got_back = exchange(back)
    volt_grad, last = call(
        adjoint_kernel,
        [VMEM, HBM, HBM, HBM],
        [(fibers, F32), ((OWNERS, 2, LANES), F32)],
        [
            pltpu.VMEM((OWNERS * CAP, LANES), F32),
            pltpu.VMEM(fibers, F32),
            pltpu.VMEM((SEGS * 8, LANES), F32),
            pltpu.SMEM(index, jnp.int32),
            pltpu.VMEM(fibers, jnp.int32),
            pltpu.VMEM((2 + 2 * STEPS, *fibers), F32),
            pltpu.VMEM(fibers, F32),
            pltpu.SemaphoreType.DMA((2,)),
            pltpu.SemaphoreType.DMA((FIB // PART,)),
            pltpu.SemaphoreType.DMA((FIB // PART,)),
        ],
        "adjoint",
        1 << 28,
        14 << 20,
        48,
        [HBM, VMEM],
    )(got_back, slots, res, seg_ids)
    ends = exchange(last)
    material_grad, cond_grad = call(
        last_kernel,
        [VMEM],
        [((LANES, LANES), F32), ((SEGS,), F32)],
        [],
        "last_sums",
        1 << 16,
        1 << 17,
    )(ends)
    return volt_grad, stress, material_grad, cond_grad


def solution(mesh):
    rows = P(AXES, None)
    return jax.shard_map(
        per_device,
        mesh=mesh,
        in_specs=(rows, rows, P(), rows, P(AXES), P(), rows),
        out_specs=(rows, rows, P(), P()),
        check_vma=False,
    )
```

```python
import jax
import jax.numpy as jnp
from jax import lax
from jax.experimental import pallas as pl
from jax.experimental.pallas import tpu as pltpu
from jax.sharding import PartitionSpec as P

SEGS = 8
STEPS = 4
LANES = 128
FIB = 128
NODES = 2048
TILES = NODES // LANES
GROUPS = FIB // 8
OWNERS = 128
CAP = 32
ROWS = 40
ELEMS = 512
AXES = ("bundle", "elem")
F32 = jnp.float32
BF16 = jnp.bfloat16
PART = 32
CHUNKS = 4
HELD = 1 << 15
RAISE = 2.0**56
TINY = 1e-37


def iota(shape, dim):
    return lax.broadcasted_iota(jnp.int32, shape, dim)


def dot(a, b):
    return jnp.dot(a, b, preferred_element_type=F32)


def dot_nt(a, b):
    return lax.dot_general(a, b, (((1,), (1,)), ((), ())), preferred_element_type=F32)


def dot_tn(a, b):
    return lax.dot_general(a, b, (((0,), (0,)), ((), ())), preferred_element_type=F32)


def onehot(mask):
    return jnp.where(mask, 1.0, 0.0)


def cut(rows):
    return [rows[:, j * LANES : (j + 1) * LANES] for j in range(TILES)]


def neighbours(v, lane):
    from_left = [pltpu.roll(x, 1, axis=1) for x in v]
    from_right = [pltpu.roll(x, LANES - 1, axis=1) for x in v]
    out = []
    for j in range(TILES):
        left = jnp.where(lane == 0, from_left[j - 1] if j else v[0], from_left[j])
        right = jnp.where(
            lane == LANES - 1, from_right[j + 1] if j < TILES - 1 else v[j], from_right[j]
        )
        out.append(left + right)
    return out


def half_cond(seg, table):
    c = jnp.full(seg.shape, 0.5 * table[0], F32)
    for s in range(1, SEGS):
        c = jnp.where(seg == s, 0.5 * table[s], c)
    return c


def start_all(pairs, sems):
    copies = [pltpu.make_async_copy(a, b, sems.at[i]) for i, (a, b) in enumerate(pairs)]
    for c in copies:
        c.start()
    return copies


def columns(j):
    return slice(j * LANES, (j + 1) * LANES)


def forward_kernel(
    table_h, volt_h, seg_h, owner_h, elem_h, send, slots,
    table, volt, seg, owner, elem, act, stage, slot_s, sems, slot_sem,
):
    parts = [slice(g * PART, (g + 1) * PART) for g in range(FIB // PART)]
    small = start_all([(owner_h, owner), (elem_h, elem), (table_h, table)], sems)
    large = start_all(
        [(a.at[p], b.at[p]) for p in parts for a, b in ((volt_h, volt), (seg_h, seg))],
        sems.at[3:],
    )
    stage[...] = jnp.zeros(stage.shape, F32)
    for c in small + large[:2]:
        c.wait()

    sub, lan = iota((LANES, LANES), 0), iota((LANES, LANES), 1)
    before = jnp.concatenate([onehot(sub < lan), jnp.ones((LANES, LANES), F32)], axis=1)
    before = before.astype(BF16)
    own_f = owner[...].astype(F32)
    own_b = own_f.astype(BF16)
    low_f = (elem[...] & 255).astype(F32)
    high_f = ((elem[...] >> 8) + 1).astype(F32)
    sub_b = sub.astype(F32).astype(BF16)
    place = iota((CAP, LANES), 0).astype(F32)
    count = jnp.zeros((LANES, LANES), F32)
    ids = jnp.zeros((OWNERS, 2 * CAP), F32)
    for b in range(GROUPS):
        mine = jnp.where(sub_b == own_b[b : b + 1, :], BF16(1), BF16(0))
        counted = dot(mine, before)
        rank = mine.astype(F32) * (counted[:, :LANES] + count)
        rank = jnp.sum(rank, axis=0, keepdims=True)
        count = count + counted[:, LANES:]
        slots[b : b + 1, :] = (own_f[b : b + 1, :] * CAP + rank).astype(jnp.int32)
        at_rank = place == rank
        named = [jnp.where(at_rank, x[b : b + 1, :], 0.0) for x in (low_f, high_f)]
        ids = ids + dot_nt(mine, jnp.concatenate(named, axis=0).astype(BF16))

    row = iota((OWNERS, 8, LANES), 1)
    again = iota((2 * CAP, 2 * LANES), 0), iota((2 * CAP, 2 * LANES), 1)
    again = again[0] == again[1] // LANES * CAP + again[1] % CAP
    ids = dot(ids.astype(BF16), onehot(again).astype(BF16))
    low_rows = jnp.broadcast_to(ids[:, None, :LANES], row.shape)
    high_rows = jnp.broadcast_to(ids[:, None, LANES:], row.shape)
    tail = jnp.where(row == 0, low_rows, jnp.where(row == 1, high_rows, 0.0))
    send[:, CAP:, :] = tail.astype(BF16)

    lane = iota((PART, LANES), 1)

    def fibers(g):
        rows = slice(g * PART, (g + 1) * PART)
        v = [1.5 * x for x in cut(volt[rows, :])]
        c = cut(half_cond(seg[rows, :], table))
        own = [0.5 - 2.0 * x for x in c]
        for _ in range(STEPS):
            both = neighbours(v, lane)
            v = [
                x * a + 0.75 * jnp.tanh(x) + k * y for x, a, k, y in zip(v, own, c, both)
            ]
        for j in range(TILES):
            act[rows, columns(j)] = jnp.tanh(v[j] * (1.0 / 1.5))

    def scatter(g):
        for f in range(g * PART, (g + 1) * PART):
            for j in range(TILES):
                slot = slot_s[f // 8, f % 8 * TILES + j]
                stage[pl.ds(slot, 1), :] = act[f : f + 1, columns(j)]

    fibers(0)
    slot_copy = pltpu.make_async_copy(slots, slot_s, slot_sem)
    slot_copy.start()
    for g in range(1, FIB // PART):
        for c in large[2 * g : 2 * g + 2]:
            c.wait()
        if g > 1:
            scatter(g - 2)
        fibers(g)
        if g == 1:
            slot_copy.wait()
    scatter(FIB // PART - 2)
    scatter(FIB // PART - 1)
    leave = []
    for m in range(CHUNKS):
        some = slice(m * OWNERS // CHUNKS, (m + 1) * OWNERS // CHUNKS)
        rows = stage[CAP * some.start : CAP * some.stop, :].astype(BF16)
        send[some, :CAP, :] = rows.reshape(-1, CAP, LANES)


def residual_kernel(table_h, volt_h, seg_h, cot_h, res, held, table, volt, seg, sems):
    pairs = [(table_h, table), (volt_h, volt), (seg_h, seg), (cot_h, held.at[:ELEMS])]
    for c in start_all(pairs, sems):
        c.wait()
    lane = iota((PART, LANES), 1)

    def fibers(g, carry):
        rows = pl.ds(pl.multiple_of(g * PART, PART), PART)
        v = cut(volt[rows, :])
        c = cut(half_cond(seg[rows, :], table))
        for j in range(TILES):
            res[0, rows, columns(j)] = c[j]
        for k in range(STEPS):
            both = neighbours(v, lane)
            new = []
            for j in range(TILES):
                t = jnp.tanh(1.5 * v[j])
                lap = both[j] - 2.0 * v[j]
                new.append(0.5 * (v[j] + t) + c[j] * lap)
                res[2 + k, rows, columns(j)] = lap
                res[2 + STEPS + k, rows, columns(j)] = 1.25 - 0.75 * t * t - 2.0 * c[j]
            v = new
        for j in range(TILES):
            t = jnp.tanh(v[j])
            res[1, rows, columns(j)] = (1.0 - t * t) * (1.0 / RAISE)
        return carry

    lax.fori_loop(0, FIB // PART, fibers, 0)


def split_two(x):
    high = x.astype(BF16)
    return high, (x - high.astype(F32)).astype(BF16)


def element_kernel(got, held, material, stress, back, cot, key_row, gsum_b, sem):
    cot_copy = pltpu.make_async_copy(held.at[:ELEMS], cot, sem)
    cot_copy.start()
    row = iota((OWNERS, 8, LANES), 1)
    src = iota((OWNERS, 8, LANES), 0)
    lan3 = iota((OWNERS, 8, LANES), 2)
    mine = src % 4 == lan3 // CAP
    tail = got[:, CAP:, :].astype(F32)
    low = jnp.where(mine & (row == 0), tail, 0.0).astype(BF16).reshape(OWNERS * 8, LANES)
    high = jnp.where(mine & (row == 1), tail, 0.0).astype(BF16).reshape(OWNERS * 8, LANES)
    pick = onehot(iota((32, OWNERS * 8), 1) // 32 == iota((32, OWNERS * 8), 0)).astype(BF16)
    low_q = dot(pick, low)
    high_q = dot(pick, high)
    sums = []
    col = iota((256, LANES), 0).astype(F32).astype(BF16)
    slots = got[:, :CAP, :].reshape(OWNERS * CAP, LANES)
    for h in range(2):
        keys = jnp.where(high_q == h + 1, low_q, -1.0).astype(BF16)
        hit = [jnp.where(col == keys[q : q + 1, :], BF16(1), BF16(0)) for q in range(32)]
        sums.append(dot(jnp.concatenate(hit, axis=1), slots))
    summed = jnp.concatenate(sums, axis=0).astype(BF16)
    out = jnp.tanh(dot(summed, material[...]))
    stress[...] = out
    cot_copy.wait()
    gpre = cot[...] * (1.0 - out * out)
    g_high, g_low = split_two(gpre)
    raised = (dot_nt(g_high, material[...]) + dot_nt(g_low, material[...])) * RAISE
    gsum_b[...] = (raised * jnp.abs(raised)).astype(BF16)
    local = dot_tn(summed, g_high) + dot_tn(summed, g_low)
    l_high = local.astype(BF16).astype(F32)
    l_low = local - l_high
    high_rows = jnp.broadcast_to(l_high[:, None, :], row.shape)
    low_rows = jnp.broadcast_to(l_low[:, None, :], row.shape)
    back[:, CAP:, :] = jnp.where(
        row == 0, high_rows, jnp.where(row == 1, low_rows, 0.0)
    ).astype(BF16)

    key_row[...] = jnp.concatenate([low_q, high_q], axis=0)
    diagonal = iota((LANES, LANES), 0) == iota((LANES, LANES), 1)
    weigh = jnp.where(iota((2 * LANES, LANES), 0) < LANES, 1.0, 256.0).astype(BF16)
    lane = iota((1, LANES), 1).astype(F32).astype(BF16)
    leave = []
    for m in range(8):
        blocks = []
        for q in range(4 * m, 4 * m + 4):
            lo = jnp.where(diagonal, key_row[q : q + 1, :], 0.0)
            hi = jnp.where(diagonal, key_row[32 + q : 33 + q, :], 0.0)
            blocks.append(jnp.concatenate([lo, hi], axis=1).astype(BF16))
        key = dot(jnp.concatenate(blocks, axis=0), weigh)
        hits = []
        for c in range(4):
            part = (key - (256.0 + 128.0 * c)).astype(BF16)
            hits.append(jnp.where(part == lane, BF16(1), BF16(0)))
        rows = dot(jnp.concatenate(hits, axis=1), gsum_b[...]).astype(BF16)
        some = slice(16 * m, 16 * m + 16)
        back[some, :CAP, :] = rows.reshape(16, CAP, LANES)


def adjoint_kernel(
    got, slots_h, res_h, seg_h, volt_h, last,
    rows_s, grads, sums, slot_s, seg, res, volt_grad, sems, res_sems, out_sems,
):
    copies = start_all([(slots_h, slot_s), (seg_h, seg)], sems)
    parts = [slice(g * PART, (g + 1) * PART) for g in range(FIB // PART)]
    arrive = start_all([(res_h.at[:, p, :], res.at[:, p, :]) for p in parts], res_sems)
    for m in range(8):
        rows = got[16 * m : 16 * (m + 1), :CAP, :].astype(F32)
        rows_s[512 * m : 512 * (m + 1), :] = rows.reshape(512, LANES)
    for c in copies:
        c.wait()
    lane = iota((PART, LANES), 1)

    def gather(g):
        for f in range(g * PART, (g + 1) * PART):
            for j in range(TILES):
                slot = slot_s[f // 8, f % 8 * TILES + j]
                grads[f : f + 1, columns(j)] = rows_s[pl.ds(slot, 1), :]

    def fibers(g):
        rows = slice(g * PART, (g + 1) * PART)
        coded = cut(grads[rows, :])
        c = cut(res[0, rows, :])
        scale = cut(res[1, rows, :])
        grad = [
            x * lax.rsqrt(jnp.maximum(jnp.abs(x), TINY)) * y for x, y in zip(coded, scale)
        ]
        total = [jnp.zeros((PART, LANES), F32)] * TILES
        for k in reversed(range(STEPS)):
            lap = cut(res[2 + k, rows, :])
            own = cut(res[2 + STEPS + k, rows, :])
            total = [t + x * d for t, x, d in zip(total, grad, lap)]
            both = neighbours([x * y for x, y in zip(grad, c)], lane)
            grad = [x * y + z for x, y, z in zip(grad, own, both)]
        ids = cut(seg[rows, :])
        for j in range(TILES):
            volt_grad[rows, columns(j)] = grad[j]
        for s in range(SEGS):
            part = jnp.where(ids[0] == s, total[0], 0.0)
            for j in range(1, TILES):
                part = part + jnp.where(ids[j] == s, total[j], 0.0)
            part = jnp.sum(part.reshape(PART // 8, 8, LANES), axis=0)
            if g:
                part = part + sums[s * 8 : s * 8 + 8, :]
            sums[s * 8 : s * 8 + 8, :] = part

    gather(0)
    gather(1)
    leave = []
    for g, p in enumerate(parts):
        arrive[g].wait()
        if g + 2 < FIB // PART:
            gather(g + 2)
        fibers(g)
        leave += start_all([(volt_grad.at[p], volt_h.at[p])], out_sems.at[g : g + 1])
    mat = jnp.sum(got[:, CAP:, :].astype(F32), axis=0)
    mat = jnp.sum(mat[:2, :], axis=0, keepdims=True)
    part = jnp.sum(sums[...].reshape(SEGS, 8, LANES), axis=1)
    part = 0.5 * jnp.sum(part, axis=1, keepdims=True)
    spot = iota((SEGS, LANES), 0) == iota((SEGS, LANES), 1)
    cond = jnp.sum(jnp.where(spot, part, 0.0), axis=0, keepdims=True)
    both = jnp.concatenate([mat, cond], axis=0)
    last[...] = jnp.broadcast_to(both[None], last.shape)
    for c in leave:
        c.wait()


def last_kernel(ends, material_grad, cond_grad):
    both = ends[...]
    material_grad[...] = both[:, 0, :]
    cond_grad[...] = jnp.sum(both, axis=0)[1, :SEGS]


VMEM = pl.BlockSpec(memory_space=pltpu.VMEM)
HBM = pl.BlockSpec(memory_space=pltpu.HBM)


def call(kernel, ins, outs, scratch, name, flops, moved, limit=48, where=None):
    return pl.pallas_call(
        kernel,
        in_specs=ins,
        out_specs=where or [VMEM] * len(outs),
        out_shape=[jax.ShapeDtypeStruct(s, t) for s, t in outs],
        scratch_shapes=scratch,
        compiler_params=pltpu.CompilerParams(vmem_limit_bytes=limit * 2**20),
        cost_estimate=pl.CostEstimate(flops=flops, bytes_accessed=moved, transcendentals=0),
        name=name,
    )


def exchange(x):
    return lax.all_to_all(x, AXES, split_axis=0, concat_axis=0, tiled=True)


def per_device(volt_start, seg_ids, cond_table, tile_owner, tile_elem, material, stress_cot):
    message = (OWNERS, ROWS, LANES)
    owner = tile_owner.reshape(GROUPS, LANES)
    elem = tile_elem.reshape(GROUPS, LANES)
    fibers = (FIB, NODES)
    index = (GROUPS, LANES)
    send, slots = call(
        forward_kernel,
        [HBM] * 5,
        [(message, BF16), (index, jnp.int32)],
        [
            pltpu.SMEM((SEGS,), F32),
            pltpu.VMEM(fibers, F32),
            pltpu.VMEM(fibers, jnp.int32),
            pltpu.VMEM(index, jnp.int32),
            pltpu.VMEM(index, jnp.int32),
            pltpu.VMEM(fibers, F32),
            pltpu.VMEM((OWNERS * CAP, LANES), F32),
            pltpu.SMEM(index, jnp.int32),
            pltpu.SemaphoreType.DMA((3 + 2 * (FIB // PART),)),
            pltpu.SemaphoreType.DMA,
        ],
        "forward",
        1 << 28,
        5 << 20,
        60,
        [VMEM, VMEM],
    )(cond_table, volt_start, seg_ids, owner, elem)
    got = exchange(send)
    res, held = call(
        residual_kernel,
        [HBM] * 4,
        [((2 + 2 * STEPS, FIB, NODES), F32), ((HELD, LANES), F32)],
        [
            pltpu.SMEM((SEGS,), F32),
            pltpu.VMEM(fibers, F32),
            pltpu.VMEM(fibers, jnp.int32),
            pltpu.SemaphoreType.DMA((4,)),
        ],
        "residuals",
        1 << 28,
        14 << 20,
        48,
        [VMEM, HBM],
    )(cond_table, volt_start, seg_ids, stress_cot)
    stress, back = call(
        element_kernel,
        [VMEM, HBM, VMEM],
        [((ELEMS, LANES), F32), (message, BF16)],
        [
            pltpu.VMEM((ELEMS, LANES), F32),
            pltpu.VMEM((64, LANES), F32),
            pltpu.VMEM((ELEMS, LANES), BF16),
            pltpu.SemaphoreType.DMA,
        ],
        "elements",
        1 << 31,
        4 << 20,
        48,
        [VMEM, VMEM],
    )(got, held, material)
    got_back = exchange(back)
    volt_grad, last = call(
        adjoint_kernel,
        [VMEM, HBM, HBM, HBM],
        [(fibers, F32), ((OWNERS, 2, LANES), F32)],
        [
            pltpu.VMEM((OWNERS * CAP, LANES), F32),
            pltpu.VMEM(fibers, F32),
            pltpu.VMEM((SEGS * 8, LANES), F32),
            pltpu.SMEM(index, jnp.int32),
            pltpu.VMEM(fibers, jnp.int32),
            pltpu.VMEM((2 + 2 * STEPS, *fibers), F32),
            pltpu.VMEM(fibers, F32),
            pltpu.SemaphoreType.DMA((2,)),
            pltpu.SemaphoreType.DMA((FIB // PART,)),
            pltpu.SemaphoreType.DMA((FIB // PART,)),
        ],
        "adjoint",
        1 << 28,
        14 << 20,
        48,
        [HBM, VMEM],
    )(got_back, slots, res, seg_ids)
    ends = exchange(last)
    material_grad, cond_grad = call(
        last_kernel,
        [VMEM],
        [((LANES, LANES), F32), ((SEGS,), F32)],
        [],
        "last_sums",
        1 << 16,
        1 << 17,
    )(ends)
    return volt_grad, stress, material_grad, cond_grad


def solution(mesh):
    rows = P(AXES, None)
    return jax.shard_map(
        per_device,
        mesh=mesh,
        in_specs=(rows, rows, P(), rows, P(AXES), P(), rows),
        out_specs=(rows, rows, P(), P()),
        check_vma=False,
    )
```

```python
import jax
import jax.numpy as jnp
from jax import lax
from jax.experimental import pallas as pl
from jax.experimental.pallas import tpu as pltpu
from jax.sharding import PartitionSpec as P

SEGS = 8
STEPS = 4
LANES = 128
FIB = 128
NODES = 2048
TILES = NODES // LANES
GROUPS = FIB // 8
OWNERS = 128
CAP = 32
ROWS = 40
ELEMS = 512
AXES = ("bundle", "elem")
F32 = jnp.float32
BF16 = jnp.bfloat16
PART = 32
CHUNKS = 4
HELD = 1 << 15
RAISE = 2.0**56
TINY = 1e-37


def iota(shape, dim):
    return lax.broadcasted_iota(jnp.int32, shape, dim)


def dot(a, b):
    return jnp.dot(a, b, preferred_element_type=F32)


def dot_nt(a, b):
    return lax.dot_general(a, b, (((1,), (1,)), ((), ())), preferred_element_type=F32)


def dot_tn(a, b):
    return lax.dot_general(a, b, (((0,), (0,)), ((), ())), preferred_element_type=F32)


def onehot(mask):
    return jnp.where(mask, 1.0, 0.0)


def cut(rows):
    return [rows[:, j * LANES : (j + 1) * LANES] for j in range(TILES)]


def neighbours(v, lane):
    from_left = [pltpu.roll(x, 1, axis=1) for x in v]
    from_right = [pltpu.roll(x, LANES - 1, axis=1) for x in v]
    out = []
    for j in range(TILES):
        left = jnp.where(lane == 0, from_left[j - 1] if j else v[0], from_left[j])
        right = jnp.where(
            lane == LANES - 1, from_right[j + 1] if j < TILES - 1 else v[j], from_right[j]
        )
        out.append(left + right)
    return out


def split_two(x):
    high = x.astype(BF16)
    return high, (x - high.astype(F32)).astype(BF16)


def stencil_weights():
    row, col = iota((2 * LANES, 2 * LANES), 0) % LANES, iota((2 * LANES, 2 * LANES), 1)
    inside = (jnp.abs(row - col) == 1) & (col < LANES)
    across = (col >= LANES) & (row + col == 2 * LANES - 1)
    across = across & ((row == 0) | (row == LANES - 1))
    return onehot(inside | across).astype(BF16)


def neighbour_sums(v, lane, weights):
    size = v[0].shape[0]
    halves = [jnp.concatenate(split_two(x), axis=1) for x in v]
    out = dot(jnp.concatenate(halves, axis=0), weights)
    mine = [out[j * size : (j + 1) * size, :LANES] for j in range(TILES)]
    gives = [out[j * size : (j + 1) * size, LANES:] for j in range(TILES)]
    first = jnp.where(lane == 0, v[0], 0.0)
    final = jnp.where(lane == LANES - 1, v[-1], 0.0)
    gives = [first, *gives, final]
    low = lane < LANES // 2
    return [mine[j] + jnp.where(low, gives[j], gives[j + 2]) for j in range(TILES)]


def half_cond(seg, table):
    c = jnp.full(seg.shape, 0.5 * table[0], F32)
    for s in range(1, SEGS):
        c = jnp.where(seg == s, 0.5 * table[s], c)
    return c


def start_all(pairs, sems):
    copies = [pltpu.make_async_copy(a, b, sems.at[i]) for i, (a, b) in enumerate(pairs)]
    for c in copies:
        c.start()
    return copies


def columns(j):
    return slice(j * LANES, (j + 1) * LANES)


def forward_kernel(
    table_h, volt_h, seg_h, owner_h, elem_h, send, slots,
    table, volt, seg, owner, elem, act, stage, slot_s, sems, slot_sem,
):
    parts = [slice(g * PART, (g + 1) * PART) for g in range(FIB // PART)]
    small = start_all([(owner_h, owner), (elem_h, elem), (table_h, table)], sems)
    large = start_all(
        [(a.at[p], b.at[p]) for p in parts for a, b in ((volt_h, volt), (seg_h, seg))],
        sems.at[3:],
    )
    stage[...] = jnp.zeros(stage.shape, F32)
    for c in small + large[:2]:
        c.wait()

    sub, lan = iota((LANES, LANES), 0), iota((LANES, LANES), 1)
    before = jnp.concatenate([onehot(sub < lan), jnp.ones((LANES, LANES), F32)], axis=1)
    before = before.astype(BF16)
    own_f = owner[...].astype(F32)
    own_b = own_f.astype(BF16)
    low_f = (elem[...] & 255).astype(F32)
    high_f = ((elem[...] >> 8) + 1).astype(F32)
    sub_b = sub.astype(F32).astype(BF16)
    place = iota((CAP, LANES), 0).astype(F32)
    count = jnp.zeros((LANES, LANES), F32)
    ids = jnp.zeros((OWNERS, 2 * CAP), F32)
    for b in range(GROUPS):
        mine = jnp.where(sub_b == own_b[b : b + 1, :], BF16(1), BF16(0))
        counted = dot(mine, before)
        rank = mine.astype(F32) * (counted[:, :LANES] + count)
        rank = jnp.sum(rank, axis=0, keepdims=True)
        count = count + counted[:, LANES:]
        slots[b : b + 1, :] = (own_f[b : b + 1, :] * CAP + rank).astype(jnp.int32)
        at_rank = place == rank
        named = [jnp.where(at_rank, x[b : b + 1, :], 0.0) for x in (low_f, high_f)]
        ids = ids + dot_nt(mine, jnp.concatenate(named, axis=0).astype(BF16))

    row = iota((OWNERS, 8, LANES), 1)
    again = iota((2 * CAP, 2 * LANES), 0), iota((2 * CAP, 2 * LANES), 1)
    again = again[0] == again[1] // LANES * CAP + again[1] % CAP
    ids = dot(ids.astype(BF16), onehot(again).astype(BF16))
    low_rows = jnp.broadcast_to(ids[:, None, :LANES], row.shape)
    high_rows = jnp.broadcast_to(ids[:, None, LANES:], row.shape)
    tail = jnp.where(row == 0, low_rows, jnp.where(row == 1, high_rows, 0.0))
    send[:, CAP:, :] = tail.astype(BF16)

    lane = iota((PART, LANES), 1)

    def fibers(g):
        rows = slice(g * PART, (g + 1) * PART)
        v = [1.5 * x for x in cut(volt[rows, :])]
        c = cut(half_cond(seg[rows, :], table))
        own = [0.5 - 2.0 * x for x in c]
        for _ in range(STEPS):
            both = neighbours(v, lane)
            v = [
                x * a + 0.75 * jnp.tanh(x) + k * y for x, a, k, y in zip(v, own, c, both)
            ]
        for j in range(TILES):
            act[rows, columns(j)] = jnp.tanh(v[j] * (1.0 / 1.5))

    def scatter(g):
        for f in range(g * PART, (g + 1) * PART):
            for j in range(TILES):
                slot = slot_s[f // 8, f % 8 * TILES + j]
                stage[pl.ds(slot, 1), :] = act[f : f + 1, columns(j)]

    fibers(0)
    slot_copy = pltpu.make_async_copy(slots, slot_s, slot_sem)
    slot_copy.start()
    for g in range(1, FIB // PART):
        for c in large[2 * g : 2 * g + 2]:
            c.wait()
        if g > 1:
            scatter(g - 2)
        fibers(g)
        if g == 1:
            slot_copy.wait()
    scatter(FIB // PART - 2)
    scatter(FIB // PART - 1)
    for m in range(CHUNKS):
        some = slice(m * OWNERS // CHUNKS, (m + 1) * OWNERS // CHUNKS)
        rows = stage[CAP * some.start : CAP * some.stop, :].astype(BF16)
        send[some, :CAP, :] = rows.reshape(-1, CAP, LANES)


def residual_kernel(table_h, volt_h, seg_h, cot_h, res, held, table, volt, seg, sems):
    pairs = [(table_h, table), (volt_h, volt), (seg_h, seg), (cot_h, held.at[:ELEMS])]
    for c in start_all(pairs, sems):
        c.wait()
    lane = iota((PART, LANES), 1)

    def fibers(g, carry):
        rows = pl.ds(pl.multiple_of(g * PART, PART), PART)
        v = cut(volt[rows, :])
        c = cut(half_cond(seg[rows, :], table))
        for j in range(TILES):
            res[0, rows, columns(j)] = c[j]
        for k in range(STEPS):
            both = neighbours(v, lane)
            new = []
            for j in range(TILES):
                t = jnp.tanh(1.5 * v[j])
                lap = both[j] - 2.0 * v[j]
                new.append(0.5 * (v[j] + t) + c[j] * lap)
                res[2 + k, rows, columns(j)] = lap
                res[2 + STEPS + k, rows, columns(j)] = 1.25 - 0.75 * t * t - 2.0 * c[j]
            v = new
        for j in range(TILES):
            t = jnp.tanh(v[j])
            res[1, rows, columns(j)] = (1.0 - t * t) * (1.0 / RAISE)
        return carry

    lax.fori_loop(0, FIB // PART, fibers, 0)


def element_kernel(
    got, held, material, stress_h, back, cot, stress, key_row, gsum_b, sem, out_sem
):
    cot_copy = pltpu.make_async_copy(held.at[:ELEMS], cot, sem)
    cot_copy.start()
    row = iota((OWNERS, 8, LANES), 1)
    src = iota((OWNERS, 8, LANES), 0)
    lan3 = iota((OWNERS, 8, LANES), 2)
    mine = src % 4 == lan3 // CAP
    tail = got[:, CAP:, :].astype(F32)
    low = jnp.where(mine & (row == 0), tail, 0.0).astype(BF16).reshape(OWNERS * 8, LANES)
    high = jnp.where(mine & (row == 1), tail, 0.0).astype(BF16).reshape(OWNERS * 8, LANES)
    pick = onehot(iota((32, OWNERS * 8), 1) // 32 == iota((32, OWNERS * 8), 0)).astype(BF16)
    low_q = dot(pick, low)
    high_q = dot(pick, high)
    sums = []
    col = iota((256, LANES), 0).astype(F32).astype(BF16)
    slots = got[:, :CAP, :].reshape(OWNERS * CAP, LANES)
    for h in range(2):
        keys = jnp.where(high_q == h + 1, low_q, -1.0).astype(BF16)
        hit = [jnp.where(col == keys[q : q + 1, :], BF16(1), BF16(0)) for q in range(32)]
        sums.append(dot(jnp.concatenate(hit, axis=1), slots))
    summed = jnp.concatenate(sums, axis=0).astype(BF16)
    out = jnp.tanh(dot(summed, material[...]))
    stress[...] = out
    leave = pltpu.make_async_copy(stress, stress_h, out_sem)
    leave.start()
    cot_copy.wait()
    gpre = cot[...] * (1.0 - out * out)
    g_high, g_low = split_two(gpre)
    raised = (dot_nt(g_high, material[...]) + dot_nt(g_low, material[...])) * RAISE
    gsum_b[...] = (raised * jnp.abs(raised)).astype(BF16)
    local = dot_tn(summed, g_high) + dot_tn(summed, g_low)
    l_high = local.astype(BF16).astype(F32)
    l_low = local - l_high
    high_rows = jnp.broadcast_to(l_high[:, None, :], row.shape)
    low_rows = jnp.broadcast_to(l_low[:, None, :], row.shape)
    back[:, CAP:, :] = jnp.where(
        row == 0, high_rows, jnp.where(row == 1, low_rows, 0.0)
    ).astype(BF16)

    key_row[...] = jnp.concatenate([low_q, high_q], axis=0)
    diagonal = iota((LANES, LANES), 0) == iota((LANES, LANES), 1)
    weigh = jnp.where(iota((2 * LANES, LANES), 0) < LANES, 1.0, 256.0).astype(BF16)
    lane = iota((1, LANES), 1).astype(F32).astype(BF16)
    for m in range(8):
        blocks = []
        for q in range(4 * m, 4 * m + 4):
            lo = jnp.where(diagonal, key_row[q : q + 1, :], 0.0)
            hi = jnp.where(diagonal, key_row[32 + q : 33 + q, :], 0.0)
            blocks.append(jnp.concatenate([lo, hi], axis=1).astype(BF16))
        key = dot(jnp.concatenate(blocks, axis=0), weigh)
        hits = []
        for c in range(4):
            part = (key - (256.0 + 128.0 * c)).astype(BF16)
            hits.append(jnp.where(part == lane, BF16(1), BF16(0)))
        rows = dot(jnp.concatenate(hits, axis=1), gsum_b[...]).astype(BF16)
        some = slice(16 * m, 16 * m + 16)
        back[some, :CAP, :] = rows.reshape(16, CAP, LANES)
    leave.wait()


def adjoint_kernel(
    got, slots_h, res_h, seg_h, volt_h, last,
    rows_s, grads, sums, slot_s, seg, res, volt_grad, sems, res_sems, out_sems,
):
    copies = start_all([(slots_h, slot_s), (seg_h, seg)], sems)
    parts = [slice(g * PART, (g + 1) * PART) for g in range(FIB // PART)]
    arrive = start_all([(res_h.at[:, p, :], res.at[:, p, :]) for p in parts], res_sems)
    for m in range(8):
        rows = got[16 * m : 16 * (m + 1), :CAP, :].astype(F32)
        rows_s[512 * m : 512 * (m + 1), :] = rows.reshape(512, LANES)
    for c in copies:
        c.wait()
    weights = stencil_weights()
    lane = iota((PART, LANES), 1)

    def gather(g):
        for f in range(g * PART, (g + 1) * PART):
            for j in range(TILES):
                slot = slot_s[f // 8, f % 8 * TILES + j]
                grads[f : f + 1, columns(j)] = rows_s[pl.ds(slot, 1), :]

    def fibers(g):
        rows = slice(g * PART, (g + 1) * PART)
        coded = cut(grads[rows, :])
        c = cut(res[0, rows, :])
        scale = cut(res[1, rows, :])
        grad = [
            x * lax.rsqrt(jnp.maximum(jnp.abs(x), TINY)) * y for x, y in zip(coded, scale)
        ]
        total = [jnp.zeros((PART, LANES), F32)] * TILES
        for k in reversed(range(STEPS)):
            lap = cut(res[2 + k, rows, :])
            own = cut(res[2 + STEPS + k, rows, :])
            total = [t + x * d for t, x, d in zip(total, grad, lap)]
            both = neighbour_sums([x * y for x, y in zip(grad, c)], lane, weights)
            grad = [x * y + z for x, y, z in zip(grad, own, both)]
        ids = cut(seg[rows, :])
        for j in range(TILES):
            volt_grad[rows, columns(j)] = grad[j]
        leave.extend(start_all([(volt_grad.at[rows], volt_h.at[rows])], out_sems.at[g : g + 1]))
        for s in range(SEGS):
            part = jnp.where(ids[0] == s, total[0], 0.0)
            for j in range(1, TILES):
                part = part + jnp.where(ids[j] == s, total[j], 0.0)
            part = jnp.sum(part.reshape(PART // 8, 8, LANES), axis=0)
            if g:
                part = part + sums[s * 8 : s * 8 + 8, :]
            sums[s * 8 : s * 8 + 8, :] = part

    gather(0)
    gather(1)
    leave = []
    for g in range(FIB // PART):
        arrive[g].wait()
        if g + 2 < FIB // PART:
            gather(g + 2)
        fibers(g)
    mat = jnp.sum(got[:, CAP:, :].astype(F32), axis=0)
    mat = jnp.sum(mat[:2, :], axis=0, keepdims=True)
    part = jnp.sum(sums[...].reshape(SEGS, 8, LANES), axis=1)
    part = 0.5 * jnp.sum(part, axis=1, keepdims=True)
    spot = iota((SEGS, LANES), 0) == iota((SEGS, LANES), 1)
    cond = jnp.sum(jnp.where(spot, part, 0.0), axis=0, keepdims=True)
    both = jnp.concatenate([mat, cond], axis=0)
    last[...] = jnp.broadcast_to(both[None], last.shape)
    for c in leave:
        c.wait()


def last_kernel(ends, material_grad, cond_grad):
    both = ends[...]
    material_grad[...] = both[:, 0, :]
    cond_grad[...] = jnp.sum(both, axis=0)[1, :SEGS]


VMEM = pl.BlockSpec(memory_space=pltpu.VMEM)
HBM = pl.BlockSpec(memory_space=pltpu.HBM)


def call(kernel, ins, outs, scratch, name, flops, moved, limit=48, where=None):
    return pl.pallas_call(
        kernel,
        in_specs=ins,
        out_specs=where or [VMEM] * len(outs),
        out_shape=[jax.ShapeDtypeStruct(s, t) for s, t in outs],
        scratch_shapes=scratch,
        compiler_params=pltpu.CompilerParams(vmem_limit_bytes=limit * 2**20),
        cost_estimate=pl.CostEstimate(flops=flops, bytes_accessed=moved, transcendentals=0),
        name=name,
    )


def exchange(x):
    return lax.all_to_all(x, AXES, split_axis=0, concat_axis=0, tiled=True)


def per_device(volt_start, seg_ids, cond_table, tile_owner, tile_elem, material, stress_cot):
    message = (OWNERS, ROWS, LANES)
    owner = tile_owner.reshape(GROUPS, LANES)
    elem = tile_elem.reshape(GROUPS, LANES)
    fibers = (FIB, NODES)
    index = (GROUPS, LANES)
    send, slots = call(
        forward_kernel,
        [HBM] * 5,
        [(message, BF16), (index, jnp.int32)],
        [
            pltpu.SMEM((SEGS,), F32),
            pltpu.VMEM(fibers, F32),
            pltpu.VMEM(fibers, jnp.int32),
            pltpu.VMEM(index, jnp.int32),
            pltpu.VMEM(index, jnp.int32),
            pltpu.VMEM(fibers, F32),
            pltpu.VMEM((OWNERS * CAP, LANES), F32),
            pltpu.SMEM(index, jnp.int32),
            pltpu.SemaphoreType.DMA((3 + 2 * (FIB // PART),)),
            pltpu.SemaphoreType.DMA,
        ],
        "forward",
        1 << 28,
        5 << 20,
        60,
        [VMEM, VMEM],
    )(cond_table, volt_start, seg_ids, owner, elem)
    got = exchange(send)
    res, held = call(
        residual_kernel,
        [HBM] * 4,
        [((2 + 2 * STEPS, FIB, NODES), F32), ((HELD, LANES), F32)],
        [
            pltpu.SMEM((SEGS,), F32),
            pltpu.VMEM(fibers, F32),
            pltpu.VMEM(fibers, jnp.int32),
            pltpu.SemaphoreType.DMA((4,)),
        ],
        "residuals",
        1 << 28,
        14 << 20,
        48,
        [VMEM, HBM],
    )(cond_table, volt_start, seg_ids, stress_cot)
    stress, back = call(
        element_kernel,
        [VMEM, HBM, VMEM],
        [((ELEMS, LANES), F32), (message, BF16)],
        [
            pltpu.VMEM((ELEMS, LANES), F32),
            pltpu.VMEM((ELEMS, LANES), F32),
            pltpu.VMEM((64, LANES), F32),
            pltpu.VMEM((ELEMS, LANES), BF16),
            pltpu.SemaphoreType.DMA,
            pltpu.SemaphoreType.DMA,
        ],
        "elements",
        1 << 31,
        4 << 20,
        48,
        [HBM, VMEM],
    )(got, held, material)
    got_back = exchange(back)
    volt_grad, last = call(
        adjoint_kernel,
        [VMEM, HBM, HBM, HBM],
        [(fibers, F32), ((OWNERS, 2, LANES), F32)],
        [
            pltpu.VMEM((OWNERS * CAP, LANES), F32),
            pltpu.VMEM(fibers, F32),
            pltpu.VMEM((SEGS * 8, LANES), F32),
            pltpu.SMEM(index, jnp.int32),
            pltpu.VMEM(fibers, jnp.int32),
            pltpu.VMEM((2 + 2 * STEPS, *fibers), F32),
            pltpu.VMEM(fibers, F32),
            pltpu.SemaphoreType.DMA((2,)),
            pltpu.SemaphoreType.DMA((FIB // PART,)),
            pltpu.SemaphoreType.DMA((FIB // PART,)),
        ],
        "adjoint",
        1 << 28,
        14 << 20,
        48,
        [HBM, VMEM],
    )(got_back, slots, res, seg_ids)
    ends = exchange(last)
    material_grad, cond_grad = call(
        last_kernel,
        [VMEM],
        [((LANES, LANES), F32), ((SEGS,), F32)],
        [],
        "last_sums",
        1 << 16,
        1 << 17,
    )(ends)
    return volt_grad, stress, material_grad, cond_grad


def solution(mesh):
    rows = P(AXES, None)
    return jax.shard_map(
        per_device,
        mesh=mesh,
        in_specs=(rows, rows, P(), rows, P(AXES), P(), rows),
        out_specs=(rows, rows, P(), P()),
        check_vma=False,
    )
```

```python
import jax
import jax.numpy as jnp
from jax import lax
from jax.experimental import pallas as pl
from jax.experimental.pallas import tpu as pltpu
from jax.sharding import PartitionSpec as P

SEGS = 8
STEPS = 4
LANES = 128
FIB = 128
NODES = 2048
TILES = NODES // LANES
GROUPS = FIB // 8
OWNERS = 128
CAP = 32
ROWS = 40
ELEMS = 512
AXES = ("bundle", "elem")
F32 = jnp.float32
BF16 = jnp.bfloat16
PART = 32
CHUNKS = 4
HELD = 1 << 15
RAISE = 2.0**56
TINY = 1e-37


def iota(shape, dim):
    return lax.broadcasted_iota(jnp.int32, shape, dim)


def dot(a, b):
    return jnp.dot(a, b, preferred_element_type=F32)


def dot_nt(a, b):
    return lax.dot_general(a, b, (((1,), (1,)), ((), ())), preferred_element_type=F32)


def dot_tn(a, b):
    return lax.dot_general(a, b, (((0,), (0,)), ((), ())), preferred_element_type=F32)


def onehot(mask):
    return jnp.where(mask, 1.0, 0.0)


def cut(rows):
    return [rows[:, j * LANES : (j + 1) * LANES] for j in range(TILES)]


def neighbours(v, lane):
    from_left = [pltpu.roll(x, 1, axis=1) for x in v]
    from_right = [pltpu.roll(x, LANES - 1, axis=1) for x in v]
    out = []
    for j in range(TILES):
        left = jnp.where(lane == 0, from_left[j - 1] if j else v[0], from_left[j])
        right = jnp.where(
            lane == LANES - 1, from_right[j + 1] if j < TILES - 1 else v[j], from_right[j]
        )
        out.append(left + right)
    return out


def split_two(x):
    high = x.astype(BF16)
    return high, (x - high.astype(F32)).astype(BF16)


def stencil_weights():
    row, col = iota((2 * LANES, 2 * LANES), 0) % LANES, iota((2 * LANES, 2 * LANES), 1)
    inside = (jnp.abs(row - col) == 1) & (col < LANES)
    across = (col >= LANES) & (row + col == 2 * LANES - 1)
    across = across & ((row == 0) | (row == LANES - 1))
    return onehot(inside | across).astype(BF16)


def neighbour_sums(v, lane, weights):
    size = v[0].shape[0]
    halves = [jnp.concatenate(split_two(x), axis=1) for x in v]
    out = dot(jnp.concatenate(halves, axis=0), weights)
    mine = [out[j * size : (j + 1) * size, :LANES] for j in range(TILES)]
    gives = [out[j * size : (j + 1) * size, LANES:] for j in range(TILES)]
    first = jnp.where(lane == 0, v[0], 0.0)
    final = jnp.where(lane == LANES - 1, v[-1], 0.0)
    gives = [first, *gives, final]
    low = lane < LANES // 2
    return [mine[j] + jnp.where(low, gives[j], gives[j + 2]) for j in range(TILES)]


def half_cond(seg, table):
    c = jnp.full(seg.shape, 0.5 * table[0], F32)
    for s in range(1, SEGS):
        c = jnp.where(seg == s, 0.5 * table[s], c)
    return c


def start_all(pairs, sems):
    copies = [pltpu.make_async_copy(a, b, sems.at[i]) for i, (a, b) in enumerate(pairs)]
    for c in copies:
        c.start()
    return copies


def columns(j):
    return slice(j * LANES, (j + 1) * LANES)


def forward_kernel(
    table_h, volt_h, seg_h, owner_h, elem_h, send, slots,
    table, volt, seg, owner, elem, act, stage, slot_s, sems, slot_sem,
):
    parts = [slice(g * PART, (g + 1) * PART) for g in range(FIB // PART)]
    small = start_all([(owner_h, owner), (elem_h, elem), (table_h, table)], sems)
    large = start_all(
        [(a.at[p], b.at[p]) for p in parts for a, b in ((volt_h, volt), (seg_h, seg))],
        sems.at[3:],
    )
    stage[...] = jnp.zeros(stage.shape, F32)
    for c in small[:2]:
        c.wait()

    sub, lan = iota((LANES, LANES), 0), iota((LANES, LANES), 1)
    before = jnp.concatenate([onehot(sub < lan), jnp.ones((LANES, LANES), F32)], axis=1)
    before = before.astype(BF16)
    own_f = owner[...].astype(F32)
    own_b = own_f.astype(BF16)
    low_f = (elem[...] & 255).astype(F32)
    high_f = ((elem[...] >> 8) + 1).astype(F32)
    sub_b = sub.astype(F32).astype(BF16)
    place = iota((CAP, LANES), 0).astype(F32)
    count = jnp.zeros((LANES, LANES), F32)
    ids = jnp.zeros((OWNERS, 2 * CAP), F32)
    for b in range(GROUPS):
        mine = jnp.where(sub_b == own_b[b : b + 1, :], BF16(1), BF16(0))
        counted = dot(mine, before)
        rank = mine.astype(F32) * (counted[:, :LANES] + count)
        rank = jnp.sum(rank, axis=0, keepdims=True)
        count = count + counted[:, LANES:]
        slots[b : b + 1, :] = (own_f[b : b + 1, :] * CAP + rank).astype(jnp.int32)
        at_rank = place == rank
        named = [jnp.where(at_rank, x[b : b + 1, :], 0.0) for x in (low_f, high_f)]
        ids = ids + dot_nt(mine, jnp.concatenate(named, axis=0).astype(BF16))

    row = iota((OWNERS, 8, LANES), 1)
    again = iota((2 * CAP, 2 * LANES), 0), iota((2 * CAP, 2 * LANES), 1)
    again = again[0] == again[1] // LANES * CAP + again[1] % CAP
    ids = dot(ids.astype(BF16), onehot(again).astype(BF16))
    low_rows = jnp.broadcast_to(ids[:, None, :LANES], row.shape)
    high_rows = jnp.broadcast_to(ids[:, None, LANES:], row.shape)
    tail = jnp.where(row == 0, low_rows, jnp.where(row == 1, high_rows, 0.0))
    send[:, CAP:, :] = tail.astype(BF16)
    for c in small[2:] + large[:2]:
        c.wait()

    lane = iota((PART, LANES), 1)

    def fibers(g):
        rows = slice(g * PART, (g + 1) * PART)
        v = [1.5 * x for x in cut(volt[rows, :])]
        c = cut(half_cond(seg[rows, :], table))
        own = [0.5 - 2.0 * x for x in c]
        for _ in range(STEPS):
            both = neighbours(v, lane)
            v = [
                x * a + 0.75 * jnp.tanh(x) + k * y for x, a, k, y in zip(v, own, c, both)
            ]
        for j in range(TILES):
            act[rows, columns(j)] = jnp.tanh(v[j] * (1.0 / 1.5))

    def scatter(g):
        for f in range(g * PART, (g + 1) * PART):
            for j in range(TILES):
                slot = slot_s[f // 8, f % 8 * TILES + j]
                stage[pl.ds(slot, 1), :] = act[f : f + 1, columns(j)]

    fibers(0)
    slot_copy = pltpu.make_async_copy(slots, slot_s, slot_sem)
    slot_copy.start()
    for g in range(1, FIB // PART):
        for c in large[2 * g : 2 * g + 2]:
            c.wait()
        if g > 1:
            scatter(g - 2)
        fibers(g)
        if g == 1:
            slot_copy.wait()
    scatter(FIB // PART - 2)
    scatter(FIB // PART - 1)
    for m in range(CHUNKS):
        some = slice(m * OWNERS // CHUNKS, (m + 1) * OWNERS // CHUNKS)
        rows = stage[CAP * some.start : CAP * some.stop, :].astype(BF16)
        send[some, :CAP, :] = rows.reshape(-1, CAP, LANES)


def residual_kernel(table_h, volt_h, seg_h, cot_h, res, held, table, volt, seg, sems):
    pairs = [(table_h, table), (volt_h, volt), (seg_h, seg), (cot_h, held.at[:ELEMS])]
    for c in start_all(pairs, sems):
        c.wait()
    lane = iota((PART, LANES), 1)

    def fibers(g, carry):
        rows = pl.ds(pl.multiple_of(g * PART, PART), PART)
        v = cut(volt[rows, :])
        c = cut(half_cond(seg[rows, :], table))
        for j in range(TILES):
            res[0, rows, columns(j)] = c[j]
        for k in range(STEPS):
            both = neighbours(v, lane)
            new = []
            for j in range(TILES):
                t = jnp.tanh(1.5 * v[j])
                lap = both[j] - 2.0 * v[j]
                new.append(0.5 * (v[j] + t) + c[j] * lap)
                res[2 + k, rows, columns(j)] = lap
                res[2 + STEPS + k, rows, columns(j)] = 1.25 - 0.75 * t * t - 2.0 * c[j]
            v = new
        for j in range(TILES):
            t = jnp.tanh(v[j])
            res[1, rows, columns(j)] = (1.0 - t * t) * (1.0 / RAISE)
        return carry

    lax.fori_loop(0, FIB // PART, fibers, 0)


def element_kernel(
    got, held, material, stress_h, back, cot, stress, key_row, gsum_b, sem, out_sem
):
    cot_copy = pltpu.make_async_copy(held.at[:ELEMS], cot, sem)
    cot_copy.start()
    row = iota((OWNERS, 8, LANES), 1)
    src = iota((OWNERS, 8, LANES), 0)
    lan3 = iota((OWNERS, 8, LANES), 2)
    mine = src % 4 == lan3 // CAP
    tail = got[:, CAP:, :].astype(F32)
    low = jnp.where(mine & (row == 0), tail, 0.0).astype(BF16).reshape(OWNERS * 8, LANES)
    high = jnp.where(mine & (row == 1), tail, 0.0).astype(BF16).reshape(OWNERS * 8, LANES)
    pick = onehot(iota((32, OWNERS * 8), 1) // 32 == iota((32, OWNERS * 8), 0)).astype(BF16)
    low_q = dot(pick, low)
    high_q = dot(pick, high)
    sums = []
    col = iota((256, LANES), 0).astype(F32).astype(BF16)
    slots = got[:, :CAP, :].reshape(OWNERS * CAP, LANES)
    for h in range(2):
        keys = jnp.where(high_q == h + 1, low_q, -1.0).astype(BF16)
        hit = [jnp.where(col == keys[q : q + 1, :], BF16(1), BF16(0)) for q in range(32)]
        sums.append(dot(jnp.concatenate(hit, axis=1), slots))
    summed = jnp.concatenate(sums, axis=0).astype(BF16)
    out = jnp.tanh(dot(summed, material[...]))
    stress[...] = out
    leave = pltpu.make_async_copy(stress, stress_h, out_sem)
    leave.start()
    cot_copy.wait()
    gpre = cot[...] * (1.0 - out * out)
    g_high, g_low = split_two(gpre)
    raised = (dot_nt(g_high, material[...]) + dot_nt(g_low, material[...])) * RAISE
    gsum_b[...] = (raised * jnp.abs(raised)).astype(BF16)
    local = dot_tn(summed, g_high) + dot_tn(summed, g_low)
    l_high = local.astype(BF16).astype(F32)
    l_low = local - l_high
    high_rows = jnp.broadcast_to(l_high[:, None, :], row.shape)
    low_rows = jnp.broadcast_to(l_low[:, None, :], row.shape)
    back[:, CAP:, :] = jnp.where(
        row == 0, high_rows, jnp.where(row == 1, low_rows, 0.0)
    ).astype(BF16)

    key_row[...] = jnp.concatenate([low_q, high_q], axis=0)
    diagonal = iota((LANES, LANES), 0) == iota((LANES, LANES), 1)
    weigh = jnp.where(iota((2 * LANES, LANES), 0) < LANES, 1.0, 256.0).astype(BF16)
    lane = iota((1, LANES), 1).astype(F32).astype(BF16)
    for m in range(8):
        blocks = []
        for q in range(4 * m, 4 * m + 4):
            lo = jnp.where(diagonal, key_row[q : q + 1, :], 0.0)
            hi = jnp.where(diagonal, key_row[32 + q : 33 + q, :], 0.0)
            blocks.append(jnp.concatenate([lo, hi], axis=1).astype(BF16))
        key = dot(jnp.concatenate(blocks, axis=0), weigh)
        hits = []
        for c in range(4):
            part = (key - (256.0 + 128.0 * c)).astype(BF16)
            hits.append(jnp.where(part == lane, BF16(1), BF16(0)))
        rows = dot(jnp.concatenate(hits, axis=1), gsum_b[...]).astype(BF16)
        some = slice(16 * m, 16 * m + 16)
        back[some, :CAP, :] = rows.reshape(16, CAP, LANES)
    leave.wait()


def adjoint_kernel(
    got, slots_h, res_h, seg_h, volt_h, last,
    rows_s, grads, sums, slot_s, seg, res, volt_grad, sems, res_sems, out_sems,
):
    copies = start_all([(slots_h, slot_s), (seg_h, seg)], sems)
    parts = [slice(g * PART, (g + 1) * PART) for g in range(FIB // PART)]
    arrive = start_all([(res_h.at[:, p, :], res.at[:, p, :]) for p in parts], res_sems)
    for m in range(8):
        rows = got[16 * m : 16 * (m + 1), :CAP, :].astype(F32)
        rows_s[512 * m : 512 * (m + 1), :] = rows.reshape(512, LANES)
    copies[0].wait()
    weights = stencil_weights()
    lane = iota((PART, LANES), 1)

    def gather(g):
        for f in range(g * PART, (g + 1) * PART):
            for j in range(TILES):
                slot = slot_s[f // 8, f % 8 * TILES + j]
                grads[f : f + 1, columns(j)] = rows_s[pl.ds(slot, 1), :]

    def fibers(g):
        rows = slice(g * PART, (g + 1) * PART)
        coded = cut(grads[rows, :])
        c = cut(res[0, rows, :])
        scale = cut(res[1, rows, :])
        grad = [
            x * lax.rsqrt(jnp.maximum(jnp.abs(x), TINY)) * y for x, y in zip(coded, scale)
        ]
        total = [jnp.zeros((PART, LANES), F32)] * TILES
        for k in reversed(range(STEPS)):
            lap = cut(res[2 + k, rows, :])
            own = cut(res[2 + STEPS + k, rows, :])
            total = [t + x * d for t, x, d in zip(total, grad, lap)]
            both = neighbour_sums([x * y for x, y in zip(grad, c)], lane, weights)
            grad = [x * y + z for x, y, z in zip(grad, own, both)]
        ids = cut(seg[rows, :])
        for j in range(TILES):
            volt_grad[rows, columns(j)] = grad[j]
        leave.extend(start_all([(volt_grad.at[rows], volt_h.at[rows])], out_sems.at[g : g + 1]))
        for s in range(SEGS):
            part = jnp.where(ids[0] == s, total[0], 0.0)
            for j in range(1, TILES):
                part = part + jnp.where(ids[j] == s, total[j], 0.0)
            part = jnp.sum(part.reshape(PART // 8, 8, LANES), axis=0)
            if g:
                part = part + sums[s * 8 : s * 8 + 8, :]
            sums[s * 8 : s * 8 + 8, :] = part

    gather(0)
    gather(1)
    leave = []
    copies[1].wait()
    for g in range(FIB // PART):
        arrive[g].wait()
        if g + 2 < FIB // PART:
            gather(g + 2)
        fibers(g)
    mat = jnp.sum(got[:, CAP:, :].astype(F32), axis=0)
    mat = jnp.sum(mat[:2, :], axis=0, keepdims=True)
    part = jnp.sum(sums[...].reshape(SEGS, 8, LANES), axis=1)
    part = 0.5 * jnp.sum(part, axis=1, keepdims=True)
    spot = iota((SEGS, LANES), 0) == iota((SEGS, LANES), 1)
    cond = jnp.sum(jnp.where(spot, part, 0.0), axis=0, keepdims=True)
    both = jnp.concatenate([mat, cond], axis=0)
    last[...] = jnp.broadcast_to(both[None], last.shape)
    for c in leave:
        c.wait()


def last_kernel(ends, material_grad, cond_grad):
    both = ends[...]
    material_grad[...] = both[:, 0, :]
    cond_grad[...] = jnp.sum(both, axis=0)[1, :SEGS]


VMEM = pl.BlockSpec(memory_space=pltpu.VMEM)
HBM = pl.BlockSpec(memory_space=pltpu.HBM)


def call(kernel, ins, outs, scratch, name, flops, moved, limit=48, where=None):
    return pl.pallas_call(
        kernel,
        in_specs=ins,
        out_specs=where or [VMEM] * len(outs),
        out_shape=[jax.ShapeDtypeStruct(s, t) for s, t in outs],
        scratch_shapes=scratch,
        compiler_params=pltpu.CompilerParams(vmem_limit_bytes=limit * 2**20),
        cost_estimate=pl.CostEstimate(flops=flops, bytes_accessed=moved, transcendentals=0),
        name=name,
    )


def exchange(x):
    return lax.all_to_all(x, AXES, split_axis=0, concat_axis=0, tiled=True)


def per_device(volt_start, seg_ids, cond_table, tile_owner, tile_elem, material, stress_cot):
    message = (OWNERS, ROWS, LANES)
    owner = tile_owner.reshape(GROUPS, LANES)
    elem = tile_elem.reshape(GROUPS, LANES)
    fibers = (FIB, NODES)
    index = (GROUPS, LANES)
    send, slots = call(
        forward_kernel,
        [HBM] * 5,
        [(message, BF16), (index, jnp.int32)],
        [
            pltpu.SMEM((SEGS,), F32),
            pltpu.VMEM(fibers, F32),
            pltpu.VMEM(fibers, jnp.int32),
            pltpu.VMEM(index, jnp.int32),
            pltpu.VMEM(index, jnp.int32),
            pltpu.VMEM(fibers, F32),
            pltpu.VMEM((OWNERS * CAP, LANES), F32),
            pltpu.SMEM(index, jnp.int32),
            pltpu.SemaphoreType.DMA((3 + 2 * (FIB // PART),)),
            pltpu.SemaphoreType.DMA,
        ],
        "forward",
        1 << 28,
        5 << 20,
        60,
        [VMEM, VMEM],
    )(cond_table, volt_start, seg_ids, owner, elem)
    got = exchange(send)
    res, held = call(
        residual_kernel,
        [HBM] * 4,
        [((2 + 2 * STEPS, FIB, NODES), F32), ((HELD, LANES), F32)],
        [
            pltpu.SMEM((SEGS,), F32),
            pltpu.VMEM(fibers, F32),
            pltpu.VMEM(fibers, jnp.int32),
            pltpu.SemaphoreType.DMA((4,)),
        ],
        "residuals",
        1 << 28,
        14 << 20,
        48,
        [VMEM, HBM],
    )(cond_table, volt_start, seg_ids, stress_cot)
    stress, back = call(
        element_kernel,
        [VMEM, HBM, VMEM],
        [((ELEMS, LANES), F32), (message, BF16)],
        [
            pltpu.VMEM((ELEMS, LANES), F32),
            pltpu.VMEM((ELEMS, LANES), F32),
            pltpu.VMEM((64, LANES), F32),
            pltpu.VMEM((ELEMS, LANES), BF16),
            pltpu.SemaphoreType.DMA,
            pltpu.SemaphoreType.DMA,
        ],
        "elements",
        1 << 31,
        4 << 20,
        48,
        [HBM, VMEM],
    )(got, held, material)
    got_back = exchange(back)
    volt_grad, last = call(
        adjoint_kernel,
        [VMEM, HBM, HBM, HBM],
        [(fibers, F32), ((OWNERS, 2, LANES), F32)],
        [
            pltpu.VMEM((OWNERS * CAP, LANES), F32),
            pltpu.VMEM(fibers, F32),
            pltpu.VMEM((SEGS * 8, LANES), F32),
            pltpu.SMEM(index, jnp.int32),
            pltpu.VMEM(fibers, jnp.int32),
            pltpu.VMEM((2 + 2 * STEPS, *fibers), F32),
            pltpu.VMEM(fibers, F32),
            pltpu.SemaphoreType.DMA((2,)),
            pltpu.SemaphoreType.DMA((FIB // PART,)),
            pltpu.SemaphoreType.DMA((FIB // PART,)),
        ],
        "adjoint",
        1 << 28,
        14 << 20,
        48,
        [HBM, VMEM],
    )(got_back, slots, res, seg_ids)
    ends = exchange(last)
    material_grad, cond_grad = call(
        last_kernel,
        [VMEM],
        [((LANES, LANES), F32), ((SEGS,), F32)],
        [],
        "last_sums",
        1 << 16,
        1 << 17,
    )(ends)
    return volt_grad, stress, material_grad, cond_grad


def solution(mesh):
    rows = P(AXES, None)
    return jax.shard_map(
        per_device,
        mesh=mesh,
        in_specs=(rows, rows, P(), rows, P(AXES), P(), rows),
        out_specs=(rows, rows, P(), P()),
        check_vma=False,
    )
```
